512 devices in a mesh: rows: 64 (over z, y), feat: 8 (over x, core).
Axes of the slice: x: 4, y: 8, z: 8, core: 2. Of those that a mesh axis runs over, the one named last changes fastest.
Arguments:
- predictions: bfloat16 [98304, 4096], P('rows', 'feat'), may hold values from -9 to 9
- targets: bfloat16 [98304, 4096], P('rows', 'feat'), may hold values from 0 to 1
- sketch_matrix: bfloat16 [32, 4096], P(None, 'feat'), may hold values from -0.0048828125 to 0.0048828125
- bin_codes: int32 [256, 98304], P('feat', 'rows'), may hold values from 0 to 255
- row_node: int32 [98304], P('rows'), may hold values from 0 to 3
- smaller: int32 [4], replicated, may hold values from 0 to 1, as said below
- split_feature: int32 [4], replicated, may hold values from 0 to 255
- split_bin: int32 [4], replicated, may hold values from 64 to 191
Outputs:
- new_predictions: bfloat16 [98304, 4096], P('rows', 'feat')
- histograms: float32 [256, 16384], P('rows', 'feat')
The draws below stay inside these ranges and needn't reach their ends.
Inputs may be any that keep to these rules, and one draw needn't show every extreme that they name: Of the nodes 2 p and 2 p + 1 exactly one has smaller equal to 1.
All inputs are finite; a program needn't handle non-finite values.
Results may differ from the reference program's by a relative error of at most 0.0034.
Values sent between devices are 32-bit elements; how exact they have to be, the bound alone decides.
A program may use at most 64 MiB of HBM per device.

```python
import jax
import jax.numpy as jnp
from jax import lax

LABELS = 4096
FEATURES = 256
BINS = 256
SKETCH = 32
NODES = 4
ROW_DEV = 1536
ROWS = 98304
SLOTS = 2
LEAVES = 8


def split_layout(key):
    code_key = jax.random.fold_in(key, 101)
    rank_key = jax.random.fold_in(key, 102)
    order_key = jax.random.fold_in(key, 103)
    feature_key = jax.random.fold_in(key, 104)
    threshold_key = jax.random.fold_in(key, 105)
    corner_key = jax.random.fold_in(key, 106)
    bin_table = jax.random.randint(code_key, (FEATURES, ROWS), 0, BINS).astype(jnp.int32)
    weights = 12 * NODES // (jnp.arange(NODES, dtype=jnp.int32) + 1)
    bounds = jnp.cumsum(weights).astype(jnp.int32)
    weight_total = sum((12 * NODES // (index + 1) for index in range(NODES)))
    picks = jax.random.randint(rank_key, (ROWS,), 0, weight_total).astype(jnp.int32)
    ranks = jnp.sum((picks[:, None] >= bounds[None, :]).astype(jnp.int32), axis=1).astype(jnp.int32)
    permuted = jax.random.permutation(order_key, NODES).astype(jnp.int32)
    node_rows = permuted[ranks].astype(jnp.int32)
    positions = jnp.arange(NODES, dtype=jnp.int32)
    corner = jax.random.randint(corner_key, (), 0, NODES).astype(jnp.int32)
    other_corner = (corner + 1) % NODES
    split_features = jax.random.randint(feature_key, (NODES,), 0, FEATURES).astype(jnp.int32)
    split_features = jnp.where(positions == corner, FEATURES - 1, jnp.where(positions == other_corner, 0, split_features)).astype(jnp.int32)
    split_bins = jax.random.randint(threshold_key, (NODES,), BINS // 4, 3 * BINS // 4).astype(jnp.int32)
    split_bins = jnp.where(positions == corner, 3 * BINS // 4 - 1, jnp.where(positions == other_corner, BINS // 4, split_bins)).astype(jnp.int32)
    feature_rows = split_features[node_rows]
    code_at = jnp.take_along_axis(bin_table, feature_rows[None, :], axis=0)[0]
    leaf_rows = (2 * node_rows + (code_at > split_bins[node_rows]).astype(jnp.int32)).astype(jnp.int32)
    return (bin_table, node_rows, split_features, split_bins, leaf_rows)


def draw_predictions(key, part):
    bin_table, node_rows, split_features, split_bins, leaf_rows = split_layout(key)
    key = jax.random.fold_in(key, 7)
    noise_key = jax.random.fold_in(key, 1)
    shift_key = jax.random.fold_in(key, 2)
    direction = (jax.random.randint(shift_key, (2 * NODES, LABELS), 0, 3) - 1).astype(jnp.float32)
    noise = 2.0 * jax.random.truncated_normal(noise_key, -3.0, 3.0, (ROWS, LABELS), jnp.float32)
    lift = 3.0
    return (noise + lift * direction[leaf_rows]).astype(jnp.bfloat16)


def draw_bin_codes(key, part):
    bin_table, node_rows, split_features, split_bins, leaf_rows = split_layout(key)
    return bin_table


def draw_row_node(key, part):
    bin_table, node_rows, split_features, split_bins, leaf_rows = split_layout(key)
    return node_rows


def draw_split_feature(key, part):
    bin_table, node_rows, split_features, split_bins, leaf_rows = split_layout(key)
    return split_features


def draw_split_bin(key, part):
    bin_table, node_rows, split_features, split_bins, leaf_rows = split_layout(key)
    return split_bins


def draw_smaller(key, part):
    choose = jax.random.randint(jax.random.fold_in(key, 17), (NODES // 2,), 0, 2)
    first = 1 - choose
    return jnp.stack([first, choose], axis=1).reshape(NODES).astype(jnp.int32)


def levels(own_key, extent, cuts, smallest, top_value):
    factor_of, own = 1.0, jax.random.fold_in(own_key, 6)
    for dim, parts in cuts:
        steps = jnp.exp(jax.random.uniform(jax.random.fold_in(own, dim), (parts,), jnp.float32, smallest / len(cuts), top_value / len(cuts)))
        factor_of = factor_of * jnp.repeat(steps, extent[dim] // parts).reshape([-1 if axis == dim else 1 for axis in range(len(extent))])
    return factor_of


def normal_values(stream_key, extent, scale, most, shards=(), kind=jnp.bfloat16):
    result = jax.random.normal(stream_key, extent, jnp.float32) * scale
    if len(shards) > 0:
        result = levels(stream_key, extent, shards, -0.22, 0.18) * result
    return jnp.clip(result, min=-most, max=most).astype(kind)


def setup_inputs(seed: int = 0) -> dict:
    key_of = jax.random.split(jax.random.key(seed), 9)
    predictions = draw_predictions(jax.random.fold_in(key_of[8], 71), 0)
    targets = jnp.clip(1.0 * jax.random.uniform(key_of[1], (ROWS, LABELS), jnp.float32) ** levels(key_of[1], (ROWS, LABELS), ((0, 64), (1, 8)), -0.2, 0.2), 0.0, 1.0).astype(jnp.bfloat16)
    sketch_matrix = normal_values(key_of[2], (SKETCH, LABELS), (LABELS * ROWS // BINS) ** -0.5, 0.0048828125, ((1, 8),))
    bin_codes = draw_bin_codes(jax.random.fold_in(key_of[8], 71), 0)
    row_node = draw_row_node(jax.random.fold_in(key_of[8], 71), 0)
    smaller = draw_smaller(jax.random.fold_in(key_of[8], 71), 0)
    split_feature = draw_split_feature(jax.random.fold_in(key_of[8], 71), 0)
    split_bin = draw_split_bin(jax.random.fold_in(key_of[8], 71), 0)
    return dict(predictions=predictions, targets=targets, sketch_matrix=sketch_matrix, bin_codes=bin_codes, row_node=row_node, smaller=smaller, split_feature=split_feature, split_bin=split_bin)


DAMPING = 1.0
SHRINKAGE = 0.5


def reference(predictions, targets, sketch_matrix, bin_codes, row_node, smaller, split_feature, split_bin):
    blocks = ROWS // ROW_DEV
    pred_blocks = predictions.reshape(blocks, ROW_DEV, LABELS)
    target_blocks = targets.reshape(blocks, ROW_DEV, LABELS)
    code_blocks = bin_codes.reshape(FEATURES, blocks, ROW_DEV).transpose(1, 0, 2)
    node_blocks = row_node.reshape(blocks, ROW_DEV)
    feat_ids = jnp.arange(FEATURES, dtype=jnp.int32)

    def step_block(carry, inputs):
        hist_acc, grad_acc, hess_acc = carry
        pred_rows, target_rows, code_rows, node_rows = inputs
        probability = jax.nn.sigmoid(pred_rows.astype(jnp.float32))
        gradient = (probability - target_rows.astype(jnp.float32)).astype(jnp.bfloat16)
        hessian = (probability * (1.0 - probability)).astype(jnp.bfloat16)
        sketch = jnp.dot(gradient, sketch_matrix.T, preferred_element_type=jnp.float32)
        slot_mask = ((node_rows // 2)[:, None] == jnp.arange(SLOTS, dtype=jnp.int32)[None, :]) & (smaller[node_rows] == 1)[:, None]
        weighted = (slot_mask.astype(jnp.float32)[:, :, None] * sketch[:, None, :]).reshape(ROW_DEV, SLOTS * SKETCH).astype(jnp.bfloat16)
        seg_ids = (code_rows * FEATURES + feat_ids[:, None]).reshape(-1)
        spread = jnp.broadcast_to(weighted.astype(jnp.float32)[None], (FEATURES, ROW_DEV, SLOTS * SKETCH)).reshape(-1, SLOTS * SKETCH)
        hist_acc = hist_acc + jax.ops.segment_sum(spread, seg_ids, num_segments=BINS * FEATURES)
        feat_row = split_feature[node_rows]
        code_at = jnp.take_along_axis(code_rows, feat_row[None, :], axis=0)[0]
        leaf_id = (2 * node_rows + (code_at > split_bin[node_rows]).astype(jnp.int32)).astype(jnp.int32)
        leaf_hot = (jnp.arange(LEAVES, dtype=jnp.int32)[:, None] == leaf_id[None, :]).astype(jnp.bfloat16)
        grad_acc = grad_acc + jnp.dot(leaf_hot, gradient, preferred_element_type=jnp.float32)
        hess_acc = hess_acc + jnp.dot(leaf_hot, hessian, preferred_element_type=jnp.float32)
        return (hist_acc, grad_acc, hess_acc), leaf_id

    start = (jnp.zeros((BINS * FEATURES, SLOTS * SKETCH), jnp.float32), jnp.zeros((LEAVES, LABELS), jnp.float32), jnp.zeros((LEAVES, LABELS), jnp.float32))
    (hist_acc, grad_sum, hess_sum), leaf_ids = lax.scan(step_block, start, (pred_blocks, target_blocks, code_blocks, node_blocks))
    values = -grad_sum / (hess_sum + DAMPING)

    def update_block(inputs):
        pred_rows, leaf_rows = inputs
        return (pred_rows.astype(jnp.float32) + SHRINKAGE * values[leaf_rows]).astype(jnp.bfloat16)

    new_predictions = lax.map(update_block, (pred_blocks, leaf_ids)).reshape(ROWS, LABELS)
    histograms = hist_acc.reshape(BINS, FEATURES * SLOTS * SKETCH)
    return new_predictions, histograms
```

```python
import functools
import math

import jax
import jax.numpy as jnp
from jax import lax
from jax.experimental import pallas as pl
from jax.experimental.pallas import tpu as pltpu
from jax.sharding import PartitionSpec as P

BINS = 256
DAMPING = 1.0
SHRINKAGE = 0.5
SIDES = 2
GROUP = 2
CHUNK = 256
BLOCK = 64
MESH = pl.DeviceIdType.MESH


def kernel(
    side,
    feat_total,
    pred_hbm,
    targ_hbm,
    sketch_ref,
    codes_ref,
    node_ref,
    smaller_ref,
    feature_ref,
    bin_ref,
    newp_hbm,
    hist_ref,
    pred,
    targ,
    grad,
    hess,
    part,
    part_in,
    sketch,
    right,
    right_in,
    weights,
    codes,
    bins,
    hist,
    ring_in,
    last_out,
    last_in,
    leaf_out,
    leaf_in,
    leaf_sum,
    leaf_sum_in,
    value_own,
    value_in,
    values,
    leaf_hot,
    newp,
    load_sem,
    store_sem,
    right_send,
    right_recv,
    part_send,
    part_recv,
    sketch_send,
    sketch_recv,
    ring_send,
    ring_recv,
    last_send,
    last_recv,
    leaf_send,
    leaf_recv,
):
    row_count, label_count = grad.shape
    chunks = row_count // CHUNK
    feats = codes_ref.shape[0]
    nodes = smaller_ref.shape[0]
    leaves = 2 * nodes
    columns = sketch_ref.shape[0]
    groups = hist.shape[0] // GROUP
    half = side // 2
    owned_bins = BINS // (side * side)
    ring_bins = BINS // side
    leaf_part = leaves // side

    here = lax.axis_index("rows")
    me_z = here // side
    me_y = here % side
    me_f = lax.axis_index("feat")

    def at_y(k):
        return {"rows": me_z * side + (me_y + k + side) % side}

    def at_z(k):
        return {"rows": ((me_z + k + side) % side) * side + me_y}

    def at_f(k):
        return {"feat": (me_f + k) % feat_total}

    def remote(src, dst, send, recv, where):
        return pltpu.make_async_remote_copy(
            src_ref=src,
            dst_ref=dst,
            send_sem=send,
            recv_sem=recv,
            device_id=where,
            device_id_type=MESH,
        )

    def loads(c):
        rows = pl.ds(c * CHUNK, CHUNK)
        return (
            pltpu.make_async_copy(pred_hbm.at[rows], pred.at[rows], load_sem.at[0, c]),
            pltpu.make_async_copy(targ_hbm.at[rows], targ.at[rows], load_sem.at[1, c]),
        )

    for c in range(chunks):
        for copy in loads(c):
            copy.start()

    barrier = pltpu.get_barrier_semaphore()
    for k in range(1, feat_total):
        pl.semaphore_signal(barrier, inc=1, device_id=at_f(k), device_id_type=MESH)
    for k in range(1, side):
        pl.semaphore_signal(barrier, inc=1, device_id=at_y(k), device_id_type=MESH)
        pl.semaphore_signal(barrier, inc=1, device_id=at_z(k), device_id_type=MESH)

    node = node_ref[...]
    right_part = jnp.zeros((1, row_count), jnp.float32)
    for n in range(nodes):
        local = feature_ref[n] - me_f * feats
        mine = (local >= 0) & (local < feats)
        row = codes_ref[pl.ds(jnp.clip(local, 0, feats - 1), 1), :]
        limit = jnp.where(mine, bin_ref[n], BINS)
        right_part += jnp.where((node == n) & (row > limit), 1.0, 0.0)
    right[...] = right_part

    codes[...] = codes_ref[...].astype(jnp.float32)
    place = lax.broadcasted_iota(jnp.int32, (BINS, 128), 0)
    major, rest = place // ring_bins, place % ring_bins
    minor, low = rest // owned_bins, rest % owned_bins
    bins[0] = ((minor * side + major) * owned_bins + low).astype(jnp.float32).astype(jnp.bfloat16)
    bins[1] = place.astype(jnp.float32).astype(jnp.bfloat16)

    def elementwise(c):
        for copy in loads(c):
            copy.wait()

        def block(b, carry):
            rows = pl.ds(pl.multiple_of(c * CHUNK + b * BLOCK, BLOCK), BLOCK)
            logits = pred[rows, :].astype(jnp.float32)
            prob = 0.5 * jnp.tanh(0.5 * logits) + 0.5
            grad[rows, :] = (prob - targ[rows, :].astype(jnp.float32)).astype(jnp.bfloat16)
            hess[rows, :] = (prob * (1.0 - prob)).astype(jnp.bfloat16)
            return carry

        lax.fori_loop(0, CHUNK // BLOCK, block, 0)
        rows = pl.ds(c * CHUNK, CHUNK)
        part[:, rows] = lax.dot_general(
            sketch_ref[...],
            grad[rows, :],
            (((1,), (1,)), ((), ())),
            preferred_element_type=jnp.float32,
        )

    def right_copy(k):
        return remote(right, right_in.at[k], right_send.at[k], right_recv.at[k], at_f(k))

    for c in range(chunks // 2):
        elementwise(c)
    pl.semaphore_wait(barrier, feat_total - 1 + 2 * (side - 1))
    for k in range(1, feat_total):
        right_copy(k).start()
    for c in range(chunks // 2, chunks):
        elementwise(c)

    piece_rows, piece_lanes = part_in.shape[1:]
    lane_parts = row_count // piece_lanes

    def piece(f):
        return (
            pl.ds(pl.multiple_of((f // lane_parts) * piece_rows, piece_rows), piece_rows),
            pl.ds(pl.multiple_of((f % lane_parts) * piece_lanes, 128), piece_lanes),
        )

    def part_copy(k):
        return remote(
            part.at[piece((me_f + k) % feat_total)],
            part_in.at[k],
            part_send.at[k],
            part_recv.at[k],
            at_f(k),
        )

    def sketch_copy(k, owner):
        return remote(
            sketch.at[piece(owner)],
            sketch.at[piece(owner)],
            sketch_send.at[k],
            sketch_recv.at[k],
            at_f(k),
        )

    for k in range(1, feat_total):
        part_copy(k).start()

    side_of = right_part
    for k in range(1, feat_total):
        right_copy(k).wait()
        side_of = side_of + right_in[k]
    leaf_id = 2 * node + (side_of > 0.5).astype(jnp.int32)
    tall = lax.broadcasted_iota(jnp.int32, (128, row_count), 0)
    hot = jnp.where((tall % leaves == leaf_id) & (tall < 3 * leaves), 1.0, 0.0)
    leaf_hot[...] = hot.T.astype(jnp.bfloat16)
    wide = hot[:leaves].astype(jnp.bfloat16)
    grad_sum = jnp.dot(wide, grad[...], preferred_element_type=jnp.float32)
    hess_sum = jnp.dot(wide, hess[...], preferred_element_type=jnp.float32)
    for i in range(side):
        leaf_out[i, :leaf_part, :] = grad_sum[i * leaf_part : (i + 1) * leaf_part]
        leaf_out[i, leaf_part:, :] = hess_sum[i * leaf_part : (i + 1) * leaf_part]

    def leaf_copy(k):
        return remote(
            leaf_out.at[(me_y + k) % side],
            leaf_in.at[k],
            leaf_send.at[0, k],
            leaf_recv.at[0, k],
            at_y(k),
        )

    def leaf_sum_copy(k):
        return remote(
            leaf_sum, leaf_sum_in.at[k], leaf_send.at[1, k], leaf_recv.at[1, k], at_z(k)
        )

    def value_copy(k):
        return remote(value_own, value_in.at[k], leaf_send.at[2, k], leaf_recv.at[2, k], at_y(k))

    for k in range(1, side):
        leaf_copy(k).start()

    mine = part[piece(me_f)]
    for k in range(1, feat_total):
        part_copy(k).wait()
        mine = mine + part_in[k]
    sketch[piece(me_f)] = mine
    for k in range(1, feat_total):
        sketch_copy(k, me_f).start()

    total = leaf_out[me_y]
    for k in range(1, side):
        leaf_copy(k).wait()
        total = total + leaf_in[k]
    leaf_sum[...] = total
    for k in range(1, side):
        leaf_sum_copy(k).start()

    for k in range(1, feat_total):
        sketch_copy(k, me_f).wait_send()
        sketch_copy(k, (me_f - k + feat_total) % feat_total).wait_recv()

    full = sketch[...]
    zeros = jnp.zeros_like(full)
    slots = []
    for s in range(nodes // 2):
        keep = jnp.zeros((1, row_count), jnp.float32)
        for n in (2 * s, 2 * s + 1):
            keep += jnp.where((node == n) & (smaller_ref[n] == 1), 1.0, 0.0)
        slots.append(full * keep)
    first = jnp.concatenate(slots + [zeros] * len(slots), axis=0)
    weights[0] = first.T.astype(jnp.bfloat16)
    second = jnp.concatenate([zeros] * len(slots) + slots, axis=0)
    weights[1] = second.T.astype(jnp.bfloat16)

    lane_tiles = row_count // 128

    def one_hot(feature, turn):
        row = codes[pl.ds(feature, 1), :]
        tile = jnp.broadcast_to(row, (16, row_count)).astype(jnp.bfloat16)
        wanted = jnp.concatenate([tile] * (BINS // 16), axis=0)
        ids = jnp.concatenate([bins[turn]] * lane_tiles, axis=1)
        return jnp.where(ids == wanted, jnp.bfloat16(1), jnp.bfloat16(0))

    def compute(u):
        turn = u % SIDES

        def pair(i, carry):
            j = u * GROUP + i
            hist[j] = jnp.dot(
                one_hot(2 * j, turn), weights[0], preferred_element_type=jnp.float32
            ) + jnp.dot(
                one_hot(2 * j + 1, turn), weights[1], preferred_element_type=jnp.float32
            )
            return carry

        lax.fori_loop(0, GROUP, pair, 0)

    def ring_place(u):
        return (1 - u % SIDES) * me_y + (u % SIDES) * me_z

    def ring_peer(u, k):
        along_y = me_z * side + (me_y + k + side) % side
        along_z = ((me_z + k + side) % side) * side + me_y
        return {"rows": (1 - u % SIDES) * along_y + (u % SIDES) * along_z}

    def ring_rows(target):
        return pl.ds(pl.multiple_of((target + side) % side * ring_bins, ring_bins), ring_bins)

    def ring_copies(u, step):
        me = ring_place(u)
        copies = []
        for way, sign in ((0, 1), (1, -1)):
            first, count = (way, 1) if step == 0 else (0, GROUP)
            pairs = GROUP // 2 if step == 0 else GROUP
            start = way * pairs if step == 0 else 0
            copies.append(
                remote(
                    hist.at[
                        pl.ds(u * GROUP + start, pairs),
                        ring_rows(me + sign * (half - step)),
                    ],
                    ring_in.at[u, way, step, pl.ds(start, pairs)],
                    ring_send.at[u, way, step],
                    ring_recv.at[u, way, step],
                    ring_peer(u, sign),
                )
            )
        return copies

    def arrived(u, way, step):
        pairs = GROUP // 2 if step == 0 else GROUP
        start = way * pairs if step == 0 else 0
        return start, pairs, ring_in[u, way, step, start : start + pairs]

    def last_copy(u, k):
        to = (1 - u % SIDES) * me_z + (u % SIDES) * me_y
        return remote(
            last_out.at[u, (to + k) % side],
            last_in.at[u, k],
            last_send.at[u, k],
            last_recv.at[u, k],
            ring_peer(u + 1, k),
        )

    def stage(u, k):
        me = ring_place(u)
        if 1 <= k <= half:
            for copy in ring_copies(u, k - 1):
                copy.wait()
        if 1 <= k < half:
            for way, sign in ((0, 1), (1, -1)):
                start, pairs, value = arrived(u, way, k - 1)
                spot = (
                    pl.ds(u * GROUP + start, pairs),
                    ring_rows(me + sign * (half - k)),
                    slice(None),
                )
                hist[spot] = hist[spot] + value
        if k < half:
            for copy in ring_copies(u, k):
                copy.start()
        if k == half:
            for way in (0, 1):
                start, pairs, value = arrived(u, way, half - 1)
                spot = (pl.ds(u * GROUP + start, pairs), ring_rows(me), slice(None))
                hist[spot] = hist[spot] + value
            total = hist[pl.ds(u * GROUP, GROUP), ring_rows(me), :]
            for i in range(side):
                last_out[u, i] = total[:, i * owned_bins : (i + 1) * owned_bins]
            for i in range(1, side):
                last_copy(u, i).start()
        if k == half + 1:
            to = (1 - u % SIDES) * me_z + (u % SIDES) * me_y
            total = last_out[u, to]
            for i in range(1, side):
                last_copy(u, i).wait()
                total = total + last_in[u, i]
            for i in range(GROUP):
                lanes = pl.ds(pl.multiple_of((u * GROUP + i) * 128, 128), 128)
                hist_ref[:, lanes] = total[i]

    def update(c):
        rows = pl.ds(pl.multiple_of(c * CHUNK, CHUNK), CHUNK)
        moved = jnp.dot(leaf_hot[rows, :], values[...], preferred_element_type=jnp.float32)
        newp[rows, :] = (pred[rows, :].astype(jnp.float32) + SHRINKAGE * moved).astype(
            jnp.bfloat16
        )
        pltpu.make_async_copy(newp.at[rows], newp_hbm.at[rows], store_sem.at[c]).start()

    stages = half + 2
    slots_total = groups + stages - 1
    update_from = slots_total - chunks

    def slot(t, carry):
        @pl.when(t < groups)
        def _():
            compute(t)

        for k in range(stages):

            @pl.when((t >= k) & (t < groups + k))
            def _(k=k):
                stage(t - k, k)

        @pl.when(t == 0)
        def _():
            total = leaf_sum[...]
            for k in range(1, side):
                leaf_sum_copy(k).wait()
                total = total + leaf_sum_in[k]
            value_own[...] = -total[:leaf_part] / (total[leaf_part:] + DAMPING)
            for k in range(1, side):
                value_copy(k).start()

        @pl.when(t == 2)
        def _():
            for k in range(1, side):
                value_copy(k).wait()
            who = lax.broadcasted_iota(jnp.int32, (leaves, label_count), 0) // leaf_part
            found = jnp.zeros((leaves, label_count), jnp.float32)
            for k in range(side):
                owner = (me_y - k + side) % side
                row = value_own[...] if k == 0 else value_in[k]
                tiled = jnp.concatenate([row] * side, axis=0)
                found = jnp.where(who == owner, tiled, found)
            high = found.astype(jnp.bfloat16)
            rest = found - high.astype(jnp.float32)
            middle = rest.astype(jnp.bfloat16)
            rest = rest - middle.astype(jnp.float32)
            three = jnp.concatenate([high.astype(jnp.float32), middle.astype(jnp.float32), rest], 0)
            pad = jnp.zeros((128 - 3 * leaves, label_count), jnp.float32)
            values[...] = jnp.concatenate([three, pad], 0).astype(jnp.bfloat16)

        @pl.when(t >= update_from)
        def _():
            update(t - update_from)

        return carry

    lax.fori_loop(0, slots_total, slot, 0)
    for c in range(chunks):
        rows = pl.ds(c * CHUNK, CHUNK)
        pltpu.make_async_copy(newp.at[rows], newp_hbm.at[rows], store_sem.at[c]).wait()


def per_device(
    side,
    feat_total,
    predictions,
    targets,
    sketch_matrix,
    bin_codes,
    row_node,
    smaller,
    split_feature,
    split_bin,
):
    row_count, label_count = predictions.shape
    columns = sketch_matrix.shape[0]
    feats = bin_codes.shape[0]
    pairs = feats // 2
    groups = pairs // GROUP
    half = side // 2
    owned_bins = BINS // (side * side)
    leaves = 2 * smaller.shape[0]
    leaf_part = leaves // side
    chunks = row_count // CHUNK
    lane_parts = max(1, feat_total * 8 // columns)
    piece = (columns * lane_parts // feat_total, row_count // lane_parts)
    vmem = pltpu.VMEM
    bf16, f32 = jnp.bfloat16, jnp.float32
    dma = pltpu.SemaphoreType.DMA
    whole = pl.BlockSpec(memory_space=pltpu.VMEM)
    scalar = pl.BlockSpec(memory_space=pltpu.SMEM)
    anywhere = pl.BlockSpec(memory_space=pl.ANY)
    return pl.pallas_call(
        functools.partial(kernel, side, feat_total),
        out_shape=(
            jax.ShapeDtypeStruct((row_count, label_count), bf16),
            jax.ShapeDtypeStruct((owned_bins, pairs * 128), f32),
        ),
        in_specs=[anywhere, anywhere, whole, whole, whole, scalar, scalar, scalar],
        out_specs=(anywhere, whole),
        scratch_shapes=[
            vmem((row_count, label_count), bf16),
            vmem((row_count, label_count), bf16),
            vmem((row_count, label_count), bf16),
            vmem((row_count, label_count), bf16),
            vmem((columns, row_count), f32),
            vmem((feat_total,) + piece, f32),
            vmem((columns, row_count), f32),
            vmem((1, row_count), f32),
            vmem((feat_total, 1, row_count), f32),
            vmem((2, row_count, 128), bf16),
            vmem((feats, row_count), f32),
            vmem((2, BINS, 128), bf16),
            vmem((pairs, BINS, 128), f32),
            vmem((groups, 2, half, GROUP, BINS // side, 128), f32),
            vmem((groups, side, GROUP, owned_bins, 128), f32),
            vmem((groups, side, GROUP, owned_bins, 128), f32),
            vmem((side, 2 * leaf_part, label_count), f32),
            vmem((side, 2 * leaf_part, label_count), f32),
            vmem((2 * leaf_part, label_count), f32),
            vmem((side, 2 * leaf_part, label_count), f32),
            vmem((leaf_part, label_count), f32),
            vmem((side, leaf_part, label_count), f32),
            vmem((128, label_count), bf16),
            vmem((row_count, 128), bf16),
            vmem((row_count, label_count), bf16),
            dma((2, chunks)),
            dma((chunks,)),
            dma((feat_total,)),
            dma((feat_total,)),
            dma((feat_total,)),
            dma((feat_total,)),
            dma((feat_total,)),
            dma((feat_total,)),
            dma((groups, 2, half)),
            dma((groups, 2, half)),
            dma((groups, side)),
            dma((groups, side)),
            dma((3, side)),
            dma((3, side)),
        ],
        compiler_params=pltpu.CompilerParams(
            collective_id=0, has_side_effects=True, vmem_limit_bytes=48 << 20
        ),
        name="boost",
    )(
        predictions,
        targets,
        sketch_matrix,
        bin_codes,
        row_node.reshape(1, row_count),
        smaller,
        split_feature,
        split_bin,
    )


def solution(mesh):
    placed = (
        P("rows", "feat"),
        P("rows", "feat"),
        P(None, "feat"),
        P("feat", "rows"),
        P("rows"),
        P(),
        P(),
        P(),
    )
    side = math.isqrt(mesh.shape["rows"])
    return jax.shard_map(
        functools.partial(per_device, side, mesh.shape["feat"]),
        mesh=mesh,
        in_specs=placed,
        out_specs=(P("rows", "feat"), P("rows", "feat")),
        check_vma=False,
    )
```

```python
import functools
import math

import jax
import jax.numpy as jnp
from jax import lax
from jax.experimental import pallas as pl
from jax.experimental.pallas import tpu as pltpu
from jax.sharding import PartitionSpec as P

BINS = 256
DAMPING = 1.0
SHRINKAGE = 0.5
GROUP = 2
RINGS = 0
LOWER = 16.0
CHUNK = 256
BLOCK = 64
MESH = pl.DeviceIdType.MESH


def kernel(
    side,
    feat_total,
    pred_hbm,
    targ_hbm,
    matrix_hbm,
    codes_hbm,
    node_hbm,
    smaller_ref,
    feature_ref,
    bin_ref,
    newp,
    hist_ref,
    pred,
    targ,
    matrix,
    codes,
    node_line,
    grad,
    hess,
    part,
    part_in,
    sketch,
    right,
    right_in,
    weights,
    lines,
    bins,
    one_hots,
    hist,
    ring_in,
    last_out,
    last_in,
    leaf_out,
    leaf_in,
    leaf_sum,
    leaf_sum_in,
    value_own,
    value_in,
    values,
    leaf_hot,
    load_sem,
    small_sem,
    right_send,
    right_recv,
    part_send,
    part_recv,
    sketch_send,
    sketch_recv,
    ring_send,
    ring_recv,
    last_send,
    last_recv,
    leaf_send,
    leaf_recv,
):
    row_count, label_count = grad.shape
    chunks = row_count // CHUNK
    feats = codes.shape[0]
    nodes = smaller_ref.shape[0]
    leaves = 2 * nodes
    groups = hist.shape[0] // GROUP
    half = side // 2
    owned_bins = BINS // (side * side)
    ring_bins = BINS // side
    leaf_part = leaves // side

    here = lax.axis_index("rows")
    me_z = here // side
    me_y = here % side
    me_f = lax.axis_index("feat")
    me_of = (me_y, me_z)

    def at_y(k):
        return {"rows": me_z * side + (me_y + k + side) % side}

    def at_z(k):
        return {"rows": ((me_z + k + side) % side) * side + me_y}

    at_of = (at_y, at_z)

    def at_f(k):
        return {"feat": (me_f + k) % feat_total}

    def remote(src, dst, send, recv, where):
        return pltpu.make_async_remote_copy(
            src_ref=src,
            dst_ref=dst,
            send_sem=send,
            recv_sem=recv,
            device_id=where,
            device_id_type=MESH,
        )

    def loads(c):
        rows = pl.ds(c * CHUNK, CHUNK)
        return (
            pltpu.make_async_copy(pred_hbm.at[rows], pred.at[rows], load_sem.at[0, c]),
            pltpu.make_async_copy(targ_hbm.at[rows], targ.at[rows], load_sem.at[1, c]),
        )

    small_loads = (
        pltpu.make_async_copy(node_hbm, node_line, small_sem.at[0]),
        pltpu.make_async_copy(codes_hbm, codes, small_sem.at[1]),
        pltpu.make_async_copy(matrix_hbm, matrix, small_sem.at[2]),
    )
    barrier = pltpu.get_barrier_semaphore()
    for k in range(1, feat_total):
        pl.semaphore_signal(barrier, inc=1, device_id=at_f(k), device_id_type=MESH)
    for k in range(1, side):
        pl.semaphore_signal(barrier, inc=1, device_id=at_y(k), device_id_type=MESH)
        pl.semaphore_signal(barrier, inc=1, device_id=at_z(k), device_id_type=MESH)
    for copy in small_loads:
        copy.start()
    for c in range(chunks):
        for copy in loads(c):
            copy.start()

    place = lax.broadcasted_iota(jnp.int32, (BINS, 128), 0)
    major, rest = place // ring_bins, place % ring_bins
    minor, low = rest // owned_bins, rest % owned_bins
    bins[0] = ((minor * side + major) * owned_bins + low).astype(jnp.float32).astype(jnp.bfloat16)
    bins[1] = place.astype(jnp.float32).astype(jnp.bfloat16)
    for copy in small_loads:
        copy.wait()

    def elementwise(c):
        for copy in loads(c):
            copy.wait()

        def block(b, carry):
            rows = pl.ds(pl.multiple_of(c * CHUNK + b * BLOCK, BLOCK), BLOCK)
            logits = pred[rows, :].astype(jnp.float32)
            prob = 0.5 * jnp.tanh(0.5 * logits) + 0.5
            grad[rows, :] = (prob - targ[rows, :].astype(jnp.float32)).astype(jnp.bfloat16)
            hess[rows, :] = (prob * (1.0 - prob)).astype(jnp.bfloat16)
            return carry

        lax.fori_loop(0, CHUNK // BLOCK, block, 0)
        rows = pl.ds(c * CHUNK, CHUNK)
        part[:, rows] = lax.dot_general(
            matrix[...],
            grad[rows, :],
            (((1,), (1,)), ((), ())),
            preferred_element_type=jnp.float32,
        )

    for c in range(chunks):
        elementwise(c)

    node = jnp.concatenate(
        [node_line[pl.ds(i * 128, 128)].reshape(1, 128) for i in range(row_count // 128)], axis=1
    )
    right_part = jnp.zeros((1, row_count), jnp.float32)
    for n in range(nodes):
        local = feature_ref[n] - me_f * feats
        mine = (local >= 0) & (local < feats)
        row = codes[pl.ds(jnp.clip(local, 0, feats - 1), 1), :]
        limit = jnp.where(mine, bin_ref[n], BINS)
        right_part += jnp.where((node == n) & (row > limit), 1.0, 0.0)
    right[...] = right_part

    piece_rows, piece_lanes = part_in.shape[1:]
    lane_parts = row_count // piece_lanes

    def piece(f):
        return (
            pl.ds(pl.multiple_of((f // lane_parts) * piece_rows, piece_rows), piece_rows),
            pl.ds(pl.multiple_of((f % lane_parts) * piece_lanes, 128), piece_lanes),
        )

    def right_copy(k):
        return remote(right, right_in.at[k], right_send.at[k], right_recv.at[k], at_f(k))

    def part_copy(k):
        return remote(
            part.at[piece((me_f + k) % feat_total)],
            part_in.at[k],
            part_send.at[k],
            part_recv.at[k],
            at_f(k),
        )

    def sketch_copy(k, owner):
        return remote(
            sketch.at[piece(owner)],
            sketch.at[piece(owner)],
            sketch_send.at[k],
            sketch_recv.at[k],
            at_f(k),
        )

    lines[...] = codes[...].astype(jnp.float32)

    def build(first, last):
        def one(f, carry):
            turn = (f // (2 * GROUP)) % 2
            row = lines[pl.ds(f, 1), :]
            tile = jnp.broadcast_to(row, (16, row_count)).astype(jnp.bfloat16)
            wanted = jnp.concatenate([tile] * (BINS // 16), axis=0)
            ids = jnp.concatenate([bins[turn]] * (row_count // 128), axis=1)
            hot = jnp.where(ids == wanted, jnp.bfloat16(1), jnp.bfloat16(0))
            one_hots[f % 2, f // 2] = hot.astype(one_hots.dtype)
            return carry

        lax.fori_loop(first, last, one, 0)

    third = feats // 4
    build(0, third)
    pl.semaphore_wait(barrier, feat_total - 1 + 2 * (side - 1))
    for k in range(1, feat_total):
        part_copy(k).start()
    for k in range(1, feat_total):
        right_copy(k).start()
    build(third, 3 * third)

    mine = part[piece(me_f)]
    for k in range(1, feat_total):
        part_copy(k).wait()
        mine = mine + part_in[k]
    sketch[piece(me_f)] = mine
    for k in range(1, feat_total):
        sketch_copy(k, me_f).start()

    side_of = right_part
    for k in range(1, feat_total):
        right_copy(k).wait()
        side_of = side_of + right_in[k]
    leaf_id = 2 * node + (side_of > 0.5).astype(jnp.int32)
    tall = lax.broadcasted_iota(jnp.int32, (128, row_count), 0)
    hot = jnp.where((tall % leaves == leaf_id) & (tall < 3 * leaves), 1.0, 0.0)
    wide = hot[:leaves].astype(jnp.bfloat16)
    grad_sum = jnp.dot(wide, grad[...], preferred_element_type=jnp.float32)
    hess_sum = jnp.dot(wide, hess[...], preferred_element_type=jnp.float32)
    for i in range(side):
        leaf_out[i, :leaf_part, :] = grad_sum[i * leaf_part : (i + 1) * leaf_part]
        leaf_out[i, leaf_part:, :] = hess_sum[i * leaf_part : (i + 1) * leaf_part]

    def leaf_copy(k):
        return remote(
            leaf_out.at[(me_y + k) % side],
            leaf_in.at[k],
            leaf_send.at[0, k],
            leaf_recv.at[0, k],
            at_y(k),
        )

    def leaf_sum_copy(k):
        return remote(
            leaf_sum, leaf_sum_in.at[k], leaf_send.at[1, k], leaf_recv.at[1, k], at_z(k)
        )

    def value_copy(k):
        return remote(value_own, value_in.at[k], leaf_send.at[2, k], leaf_recv.at[2, k], at_y(k))

    for k in range(1, side):
        leaf_copy(k).start()
    leaf_hot[...] = hot.T.astype(jnp.bfloat16)
    build(3 * third, feats)

    for k in range(1, feat_total):
        sketch_copy(k, me_f).wait_send()
        sketch_copy(k, (me_f - k + feat_total) % feat_total).wait_recv()

    full = sketch[...]
    slots = []
    for s in range(nodes // 2):
        keep = jnp.zeros((1, row_count), jnp.float32)
        for n in (2 * s, 2 * s + 1):
            keep += jnp.where((node == n) & (smaller_ref[n] == 1), 1.0, 0.0)
        slots.append(full * keep)
    picked = jnp.concatenate(slots, axis=0).astype(jnp.bfloat16).astype(jnp.float32)
    most = jnp.max(jnp.abs(picked), axis=(0, 1), keepdims=True)
    power = jnp.floor(jnp.log2(jnp.maximum(most, 1e-30)))
    scaled = picked * jnp.exp2(7.0 - power)
    upper = scaled.astype(jnp.bfloat16).astype(weights.dtype).astype(jnp.float32)
    lower = (scaled - upper) * LOWER
    empty = jnp.zeros_like(picked)
    for i in (0, 1):
        for j, term in enumerate((upper, lower)):
            both = (term, empty) if i == 0 else (empty, term)
            turned = jnp.concatenate(both, axis=0).T.astype(jnp.bfloat16)
            weights[i, :, j * 128 : (j + 1) * 128] = turned.astype(weights.dtype)
    unscale = jnp.exp2(power - 7.0)

    def pairs_of(g):
        return pl.ds(g * GROUP, GROUP)

    def compute(g):
        total = None
        for i in (0, 1):
            left = one_hots[i, pairs_of(g)].reshape(GROUP * BINS, row_count)
            product = jnp.dot(left, weights[i], preferred_element_type=jnp.float32)
            total = product if total is None else total + product
        total = (total[:, :128] + total[:, 128:] * (1.0 / LOWER)) * unscale
        hist[pairs_of(g)] = total.reshape(GROUP, BINS, 128)

    def rows_of(target):
        return pl.ds(pl.multiple_of((target + side) % side * ring_bins, ring_bins), ring_bins)

    def ring_range(way, step):
        return (way * (GROUP // 2), GROUP // 2) if step == 0 else (0, GROUP)

    def ring_copy(g, way, step):
        sign = 1 - 2 * way
        start, count = ring_range(way, step)
        return remote(
            hist.at[
                pl.ds(g * GROUP + start, count),
                rows_of(me_of[g % 2] + sign * (half - step)),
            ],
            ring_in.at[g, way, step, pl.ds(start, count)],
            ring_send.at[g, way, step],
            ring_recv.at[g, way, step],
            at_of[g % 2](sign),
        )

    def ring_step(g, k):
        for way in (0, 1):
            if k > 0:
                ring_copy(g, way, k - 1).wait()
                start, count = ring_range(way, k - 1)
                spot = (
                    pl.ds(g * GROUP + start, count),
                    rows_of(me_of[g % 2] + (1 - 2 * way) * (half - k)),
                    slice(None),
                )
                hist[spot] = hist[spot] + ring_in[g, way, k - 1, start : start + count]
            if k < half:
                ring_copy(g, way, k).start()

    relay = max(1, half // 2)

    def relay_copy(g, way, d):
        sign = 1 - 2 * way
        start, count = ring_range(way, half - d)
        return remote(
            hist.at[pl.ds(g * GROUP + start, count), rows_of(me_of[g % 2] + sign * d)],
            ring_in.at[g, way, d - 1, pl.ds(start, count)],
            ring_send.at[g, way, d - 1],
            ring_recv.at[g, way, d - 1],
            at_of[g % 2](sign * (d - relay if d > relay else d)),
        )

    def relay_take(g, way, d, target):
        relay_copy(g, way, d).wait()
        start, count = ring_range(way, half - d)
        spot = (pl.ds(g * GROUP + start, count), rows_of(target), slice(None))
        hist[spot] = hist[spot] + ring_in[g, way, d - 1, start : start + count]

    def relay_start(g):
        for d in range(half, 0, -1):
            if d != relay or relay == half:
                for way in (0, 1):
                    relay_copy(g, way, d).start()

    def relay_pass(g):
        if relay < half:
            for way, sign in ((0, 1), (1, -1)):
                for d in range(half, relay, -1):
                    relay_take(g, way, d, me_of[g % 2] + sign * relay)
                relay_copy(g, way, relay).start()

    def relay_end(g):
        for d in range(1, relay + 1):
            for way in (0, 1):
                relay_take(g, way, d, me_of[g % 2])

    by_distance = sorted(range(1, side), key=lambda k: -min(k, side - k))

    def last_copy(g, k):
        return remote(
            last_out.at[g, (me_of[1 - g % 2] + k) % side],
            last_in.at[g, k],
            last_send.at[g, k],
            last_recv.at[g, k],
            at_of[1 - g % 2](k),
        )

    def finish(g):
        if g < RINGS:
            ring_step(g, half)
        else:
            relay_end(g)
        total = hist[pairs_of(g), rows_of(me_of[g % 2]), :]
        for i in range(side):
            last_out[g, i] = total[:, i * owned_bins : (i + 1) * owned_bins]
        for k in by_distance:
            last_copy(g, k).start()

    def collect(g):
        total = last_out[g, me_of[1 - g % 2]]
        for k in range(1, side):
            last_copy(g, k).wait()
            total = total + last_in[g, k]
        for i in range(GROUP):
            hist_ref[:, (g * GROUP + i) * 128 : (g * GROUP + i + 1) * 128] = total[i]

    def leaf_first():
        total = leaf_out[me_y]
        for k in range(1, side):
            leaf_copy(k).wait()
            total = total + leaf_in[k]
        leaf_sum[...] = total
        for k in range(1, side):
            leaf_sum_copy(k).start()

    def leaf_second():
        total = leaf_sum[...]
        for k in range(1, side):
            leaf_sum_copy(k).wait()
            total = total + leaf_sum_in[k]
        value_own[...] = -total[:leaf_part] / (total[leaf_part:] + DAMPING)
        for k in range(1, side):
            value_copy(k).start()

    def leaf_third():
        for k in range(1, side):
            value_copy(k).wait()
        who = lax.broadcasted_iota(jnp.int32, (leaves, label_count), 0) // leaf_part
        found = jnp.zeros((leaves, label_count), jnp.float32)
        for k in range(side):
            owner = (me_y - k + side) % side
            row = value_own[...] if k == 0 else value_in[k]
            tiled = jnp.concatenate([row] * side, axis=0)
            found = jnp.where(who == owner, tiled, found)
        high = found.astype(jnp.bfloat16).astype(jnp.float32)
        rest = found - high
        middle = rest.astype(jnp.bfloat16).astype(jnp.float32)
        pad = jnp.zeros((128 - 3 * leaves, label_count), jnp.float32)
        values[...] = jnp.concatenate([high, middle, rest - middle, pad], 0).astype(jnp.bfloat16)

    def update(c):
        rows = pl.ds(c * CHUNK, CHUNK)
        moved = jnp.dot(leaf_hot[rows, :], values[...], preferred_element_type=jnp.float32)
        newp[rows, :] = (pred[rows, :].astype(jnp.float32) + SHRINKAGE * moved).astype(
            jnp.bfloat16
        )

    plan = [(3.0, leaf_first), (8.5, leaf_second), (13.5, leaf_third)]
    for g in range(groups):
        compute(g)
        ready = 0.6 * (g + 1)
        if g < RINGS:
            ring_step(g, 0)
            for k in range(1, half):
                plan.append((ready + 3.6 * k, functools.partial(ring_step, g, k)))
            ready += 3.6 * half
        else:
            relay_start(g)
            plan.append((ready + 5.0, functools.partial(relay_pass, g)))
            ready += 10.0
        plan.append((ready, functools.partial(finish, g)))
        plan.append((max(ready, 18.0) + 6.0, functools.partial(collect, g)))
    for c in range(chunks):
        plan.append((23.9, functools.partial(update, c)))
    for _, step in sorted(plan, key=lambda item: item[0]):
        step()


def per_device(
    side,
    feat_total,
    predictions,
    targets,
    sketch_matrix,
    bin_codes,
    row_node,
    smaller,
    split_feature,
    split_bin,
):
    row_count, label_count = predictions.shape
    columns = sketch_matrix.shape[0]
    feats = bin_codes.shape[0]
    pairs = feats // 2
    groups = pairs // GROUP
    half = side // 2
    owned_bins = BINS // (side * side)
    leaves = 2 * smaller.shape[0]
    leaf_part = leaves // side
    chunks = row_count // CHUNK
    lane_parts = max(1, feat_total * 8 // columns)
    piece = (columns * lane_parts // feat_total, row_count // lane_parts)
    vmem = pltpu.VMEM
    bf16, f32, i32, f8 = jnp.bfloat16, jnp.float32, jnp.int32, jnp.float8_e4m3fn
    dma = pltpu.SemaphoreType.DMA
    whole = pl.BlockSpec(memory_space=pltpu.VMEM)
    scalar = pl.BlockSpec(memory_space=pltpu.SMEM)
    far = pl.BlockSpec(memory_space=pltpu.HBM)
    wide_shape = (row_count, label_count)
    return pl.pallas_call(
        functools.partial(kernel, side, feat_total),
        out_shape=(
            jax.ShapeDtypeStruct(wide_shape, bf16),
            jax.ShapeDtypeStruct((owned_bins, pairs * 128), f32),
        ),
        in_specs=[far] * 5 + [scalar] * 3,
        out_specs=(whole, whole),
        scratch_shapes=[
            vmem(wide_shape, bf16),
            vmem(wide_shape, bf16),
            vmem((columns, label_count), bf16),
            vmem((feats, row_count), i32),
            vmem((row_count,), i32),
            vmem(wide_shape, bf16),
            vmem(wide_shape, bf16),
            vmem((columns, row_count), f32),
            vmem((feat_total,) + piece, f32),
            vmem((columns, row_count), f32),
            vmem((1, row_count), f32),
            vmem((feat_total, 1, row_count), f32),
            vmem((2, row_count, 256), f8),
            vmem((feats, row_count), f32),
            vmem((2, BINS, 128), bf16),
            vmem((2, pairs, BINS, row_count), f8),
            vmem((pairs, BINS, 128), f32),
            vmem((groups, 2, half, GROUP, BINS // side, 128), f32),
            vmem((groups, side, GROUP, owned_bins, 128), f32),
            vmem((groups, side, GROUP, owned_bins, 128), f32),
            vmem((side, 2 * leaf_part, label_count), f32),
            vmem((side, 2 * leaf_part, label_count), f32),
            vmem((2 * leaf_part, label_count), f32),
            vmem((side, 2 * leaf_part, label_count), f32),
            vmem((leaf_part, label_count), f32),
            vmem((side, leaf_part, label_count), f32),
            vmem((128, label_count), bf16),
            vmem((row_count, 128), bf16),
            dma((2, chunks)),
            dma((3,)),
            dma((feat_total,)),
            dma((feat_total,)),
            dma((feat_total,)),
            dma((feat_total,)),
            dma((feat_total,)),
            dma((feat_total,)),
            dma((groups, 2, half)),
            dma((groups, 2, half)),
            dma((groups, side)),
            dma((groups, side)),
            dma((3, side)),
            dma((3, side)),
        ],
        compiler_params=pltpu.CompilerParams(
            collective_id=0, has_side_effects=True, vmem_limit_bytes=62 << 20
        ),
        name="boost",
    )(
        predictions,
        targets,
        sketch_matrix,
        bin_codes,
        row_node,
        smaller,
        split_feature,
        split_bin,
    )


def solution(mesh):
    placed = (
        P("rows", "feat"),
        P("rows", "feat"),
        P(None, "feat"),
        P("feat", "rows"),
        P("rows"),
        P(),
        P(),
        P(),
    )
    side = math.isqrt(mesh.shape["rows"])
    return jax.shard_map(
        functools.partial(per_device, side, mesh.shape["feat"]),
        mesh=mesh,
        in_specs=placed,
        out_specs=(P("rows", "feat"), P("rows", "feat")),
        check_vma=False,
    )
```

```python
import functools
import math

import jax
import jax.numpy as jnp
from jax import lax
from jax.experimental import pallas as pl
from jax.experimental.pallas import tpu as pltpu
from jax.sharding import PartitionSpec as P

BINS = 256
DAMPING = 1.0
SHRINKAGE = 0.5
UNIT = 2
GROUPS = ((0, 0, 2), (1, 0, 2), (0, 2, 4), (1, 2, 4), (0, 6, 2), (1, 6, 2))
WIDEST = 4
LOWER = 16.0
CHUNK = 256
BLOCK = 64
MESH = pl.DeviceIdType.MESH


def kernel(
    side,
    feat_total,
    pred_hbm,
    targ_hbm,
    matrix_hbm,
    codes_hbm,
    node_hbm,
    smaller_ref,
    feature_ref,
    bin_ref,
    newp_hbm,
    hist_ref,
    pred,
    targ,
    matrix,
    codes,
    node_line,
    grad,
    hess,
    part,
    part_in,
    sketch,
    right,
    right_in,
    weights,
    lines,
    bins,
    one_hots,
    hist,
    ring_in,
    last_out,
    last_in,
    leaf_out,
    leaf_in,
    leaf_sum,
    leaf_sum_in,
    value_own,
    value_in,
    values,
    leaf_hot,
    newp,
    load_sem,
    small_sem,
    store_sem,
    right_send,
    right_recv,
    part_send,
    part_recv,
    sketch_send,
    sketch_recv,
    ring_send,
    ring_recv,
    last_send,
    last_recv,
    leaf_send,
    leaf_recv,
):
    row_count, label_count = grad.shape
    chunks = row_count // CHUNK
    feats = codes.shape[0]
    nodes = smaller_ref.shape[0]
    leaves = 2 * nodes
    per_axis = hist.shape[0] // 2
    half = side // 2
    owned_bins = BINS // (side * side)
    ring_bins = BINS // side
    leaf_part = leaves // side

    here = lax.axis_index("rows")
    me_z = here // side
    me_y = here % side
    me_f = lax.axis_index("feat")
    me_of = (me_y, me_z)

    def at_y(k):
        return {"rows": me_z * side + (me_y + k + side) % side}

    def at_z(k):
        return {"rows": ((me_z + k + side) % side) * side + me_y}

    at_of = (at_y, at_z)

    def at_f(k):
        return {"feat": (me_f + k) % feat_total}

    def remote(src, dst, send, recv, where):
        return pltpu.make_async_remote_copy(
            src_ref=src,
            dst_ref=dst,
            send_sem=send,
            recv_sem=recv,
            device_id=where,
            device_id_type=MESH,
        )

    def loads(c):
        rows = pl.ds(c * CHUNK, CHUNK)
        return (
            pltpu.make_async_copy(pred_hbm.at[rows], pred.at[rows], load_sem.at[0, c]),
            pltpu.make_async_copy(targ_hbm.at[rows], targ.at[rows], load_sem.at[1, c]),
        )

    small_loads = (
        pltpu.make_async_copy(node_hbm, node_line, small_sem.at[0]),
        pltpu.make_async_copy(codes_hbm, codes, small_sem.at[1]),
        pltpu.make_async_copy(matrix_hbm, matrix, small_sem.at[2]),
    )
    barrier = pltpu.get_barrier_semaphore()
    for k in range(1, feat_total):
        pl.semaphore_signal(barrier, inc=1, device_id=at_f(k), device_id_type=MESH)
    for k in range(1, side):
        pl.semaphore_signal(barrier, inc=1, device_id=at_y(k), device_id_type=MESH)
        pl.semaphore_signal(barrier, inc=1, device_id=at_z(k), device_id_type=MESH)
    for copy in small_loads:
        copy.start()
    for c in range(chunks):
        for copy in loads(c):
            copy.start()

    place = lax.broadcasted_iota(jnp.int32, (BINS, 128), 0)
    major, rest = place // ring_bins, place % ring_bins
    minor, low = rest // owned_bins, rest % owned_bins
    bins[0] = ((minor * side + major) * owned_bins + low).astype(jnp.float32).astype(jnp.bfloat16)
    bins[1] = place.astype(jnp.float32).astype(jnp.bfloat16)
    for copy in small_loads:
        copy.wait()

    def elementwise(c):
        for copy in loads(c):
            copy.wait()

        def block(b, carry):
            rows = pl.ds(pl.multiple_of(c * CHUNK + b * BLOCK, BLOCK), BLOCK)
            logits = pred[rows, :].astype(jnp.float32)
            prob = 0.5 * jnp.tanh(0.5 * logits) + 0.5
            grad[rows, :] = (prob - targ[rows, :].astype(jnp.float32)).astype(jnp.bfloat16)
            hess[rows, :] = (prob * (1.0 - prob)).astype(jnp.bfloat16)
            return carry

        lax.fori_loop(0, CHUNK // BLOCK, block, 0)
        rows = pl.ds(c * CHUNK, CHUNK)
        part[:, rows] = lax.dot_general(
            matrix[...],
            grad[rows, :],
            (((1,), (1,)), ((), ())),
            preferred_element_type=jnp.float32,
        )

    for c in range(chunks):
        elementwise(c)

    node = jnp.concatenate(
        [node_line[pl.ds(i * 128, 128)].reshape(1, 128) for i in range(row_count // 128)], axis=1
    )
    right_part = jnp.zeros((1, row_count), jnp.float32)
    for n in range(nodes):
        local = feature_ref[n] - me_f * feats
        mine = (local >= 0) & (local < feats)
        row = codes[pl.ds(jnp.clip(local, 0, feats - 1), 1), :]
        limit = jnp.where(mine, bin_ref[n], BINS)
        right_part += jnp.where((node == n) & (row > limit), 1.0, 0.0)
    right[...] = right_part

    piece_rows, piece_lanes = part_in.shape[1:]
    lane_parts = row_count // piece_lanes

    def piece(f):
        return (
            pl.ds(pl.multiple_of((f // lane_parts) * piece_rows, piece_rows), piece_rows),
            pl.ds(pl.multiple_of((f % lane_parts) * piece_lanes, 128), piece_lanes),
        )

    def right_copy(k):
        return remote(right, right_in.at[k], right_send.at[k], right_recv.at[k], at_f(k))

    def part_copy(k):
        return remote(
            part.at[piece((me_f + k) % feat_total)],
            part_in.at[k],
            part_send.at[k],
            part_recv.at[k],
            at_f(k),
        )

    def sketch_copy(k, owner):
        return remote(
            sketch.at[piece(owner)],
            sketch.at[piece(owner)],
            sketch_send.at[k],
            sketch_recv.at[k],
            at_f(k),
        )

    lines[...] = codes[...].astype(jnp.float32)

    def build(first, last):
        def one(f, carry):
            unit = f // (2 * UNIT)
            turn = unit % 2
            slot = turn * per_axis + unit // 2 * UNIT + f // 2 % UNIT
            row = lines[pl.ds(f, 1), :]
            tile = jnp.broadcast_to(row, (16, row_count)).astype(jnp.bfloat16)
            wanted = jnp.concatenate([tile] * (BINS // 16), axis=0)
            ids = jnp.concatenate([bins[turn]] * (row_count // 128), axis=1)
            hot = jnp.where(ids == wanted, jnp.bfloat16(1), jnp.bfloat16(0))
            one_hots[f % 2, slot] = hot.astype(one_hots.dtype)
            return carry

        lax.fori_loop(first, last, one, 0)

    third = feats // 4
    build(0, third)
    pl.semaphore_wait(barrier, feat_total - 1 + 2 * (side - 1))
    for k in range(1, feat_total):
        part_copy(k).start()
    for k in range(1, feat_total):
        right_copy(k).start()
    build(third, 3 * third)

    mine = part[piece(me_f)]
    for k in range(1, feat_total):
        part_copy(k).wait()
        mine = mine + part_in[k]
    sketch[piece(me_f)] = mine
    for k in range(1, feat_total):
        sketch_copy(k, me_f).start()

    side_of = right_part
    for k in range(1, feat_total):
        right_copy(k).wait()
        side_of = side_of + right_in[k]
    leaf_id = 2 * node + (side_of > 0.5).astype(jnp.int32)
    tall = lax.broadcasted_iota(jnp.int32, (128, row_count), 0)
    hot = jnp.where((tall % leaves == leaf_id) & (tall < 3 * leaves), 1.0, 0.0)
    wide = hot[:leaves].astype(jnp.bfloat16)
    grad_sum = jnp.dot(wide, grad[...], preferred_element_type=jnp.float32)
    hess_sum = jnp.dot(wide, hess[...], preferred_element_type=jnp.float32)
    for i in range(side):
        leaf_out[i, :leaf_part, :] = grad_sum[i * leaf_part : (i + 1) * leaf_part]
        leaf_out[i, leaf_part:, :] = hess_sum[i * leaf_part : (i + 1) * leaf_part]

    def leaf_copy(k):
        return remote(
            leaf_out.at[(me_y + k) % side],
            leaf_in.at[k],
            leaf_send.at[0, k],
            leaf_recv.at[0, k],
            at_y(k),
        )

    def leaf_sum_copy(k):
        return remote(
            leaf_sum, leaf_sum_in.at[k], leaf_send.at[1, k], leaf_recv.at[1, k], at_z(k)
        )

    def value_copy(k):
        return remote(value_own, value_in.at[k], leaf_send.at[2, k], leaf_recv.at[2, k], at_y(k))

    for k in range(1, side):
        leaf_copy(k).start()
    leaf_hot[...] = hot.T.astype(jnp.bfloat16)
    build(3 * third, feats)

    for k in range(1, feat_total):
        sketch_copy(k, me_f).wait_send()
        sketch_copy(k, (me_f - k + feat_total) % feat_total).wait_recv()

    full = sketch[...]
    slots = []
    for s in range(nodes // 2):
        keep = jnp.zeros((1, row_count), jnp.float32)
        for n in (2 * s, 2 * s + 1):
            keep += jnp.where((node == n) & (smaller_ref[n] == 1), 1.0, 0.0)
        slots.append(full * keep)
    picked = jnp.concatenate(slots, axis=0).astype(jnp.bfloat16).astype(jnp.float32)
    most = jnp.max(jnp.abs(picked), axis=(0, 1), keepdims=True)
    power = jnp.floor(jnp.log2(jnp.maximum(most, 1e-30)))
    scaled = picked * jnp.exp2(7.0 - power)
    upper = scaled.astype(jnp.bfloat16).astype(weights.dtype).astype(jnp.float32)
    lower = (scaled - upper) * LOWER
    turned = jnp.concatenate([upper, lower], axis=0).T
    swapped = pltpu.roll(turned, 64, 1)
    left_half = lax.broadcasted_iota(jnp.int32, turned.shape, 1) < 64
    tables = (
        (jnp.where(left_half, turned, 0.0), jnp.where(left_half, swapped, 0.0)),
        (jnp.where(left_half, 0.0, swapped), jnp.where(left_half, 0.0, turned)),
    )
    for i in (0, 1):
        for j in (0, 1):
            table = tables[i][j].astype(jnp.bfloat16)
            weights[i, :, j * 128 : (j + 1) * 128] = table.astype(weights.dtype)
    unscale = jnp.exp2(power - 7.0)

    axis_of = [axis for axis, _, _ in GROUPS]
    size_of = [size for _, _, size in GROUPS]
    start_of = [axis * per_axis + first for axis, first, _ in GROUPS]

    def pairs_of(g):
        return pl.ds(start_of[g], size_of[g])

    def compute(g):
        total = None
        for i in (0, 1):
            left = one_hots[i, pairs_of(g)].reshape(size_of[g] * BINS, row_count)
            product = jnp.dot(left, weights[i], preferred_element_type=jnp.float32)
            total = product if total is None else total + product
        total = (total[:, :128] + total[:, 128:] * (1.0 / LOWER)) * unscale
        hist[pairs_of(g)] = total.reshape(size_of[g], BINS, 128)

    def rows_of(target):
        return pl.ds(pl.multiple_of((target + side) % side * ring_bins, ring_bins), ring_bins)

    def pair_range(g, way, d):
        size = size_of[g]
        return (way * (size // 2), size // 2) if d == half else (0, size)

    relay = max(1, half // 2)

    def relay_copy(g, way, d):
        sign = 1 - 2 * way
        start, count = pair_range(g, way, d)
        return remote(
            hist.at[pl.ds(start_of[g] + start, count), rows_of(me_of[axis_of[g]] + sign * d)],
            ring_in.at[g, way, d - 1, pl.ds(start, count)],
            ring_send.at[g, way, d - 1],
            ring_recv.at[g, way, d - 1],
            at_of[axis_of[g]](sign * (d - relay if d > relay else d)),
        )

    def relay_take(g, way, d, target):
        relay_copy(g, way, d).wait()
        start, count = pair_range(g, way, d)
        spot = (pl.ds(start_of[g] + start, count), rows_of(target), slice(None))
        hist[spot] = hist[spot] + ring_in[g, way, d - 1, start : start + count]

    def relay_start(g):
        for d in range(half, 0, -1):
            if d != relay or relay == half:
                for way in (0, 1):
                    relay_copy(g, way, d).start()

    def relay_pass(g):
        if relay < half:
            for way, sign in ((0, 1), (1, -1)):
                for d in range(half, relay, -1):
                    relay_take(g, way, d, me_of[axis_of[g]] + sign * relay)
                relay_copy(g, way, relay).start()

    def relay_end(g):
        for d in range(1, relay + 1):
            for way in (0, 1):
                relay_take(g, way, d, me_of[axis_of[g]])

    by_distance = sorted(range(1, side), key=lambda k: -min(k, side - k))

    def last_copy(c, k):
        return remote(
            last_out.at[c, (me_of[1 - c] + k) % side],
            last_in.at[c, k],
            last_send.at[c, k],
            last_recv.at[c, k],
            at_of[1 - c](k),
        )

    def finish(g):
        relay_end(g)
        total = hist[pairs_of(g), rows_of(me_of[axis_of[g]]), :]
        spot = pl.ds(GROUPS[g][1], size_of[g])
        for i in range(side):
            last_out[axis_of[g], i, spot] = total[:, i * owned_bins : (i + 1) * owned_bins]

    def last_start(c):
        for k in by_distance:
            last_copy(c, k).start()

    def collect(c):
        total = last_out[c, me_of[1 - c]]
        for k in range(1, side):
            last_copy(c, k).wait()
            total = total + last_in[c, k]
        for i in range(total.shape[0]):
            pair = (i // UNIT * 2 + c) * UNIT + i % UNIT
            hist_ref[:, pair * 128 : (pair + 1) * 128] = total[i]

    def leaf_first():
        total = leaf_out[me_y]
        for k in range(1, side):
            leaf_copy(k).wait()
            total = total + leaf_in[k]
        leaf_sum[...] = total
        for k in range(1, side):
            leaf_sum_copy(k).start()

    def leaf_second():
        total = leaf_sum[...]
        for k in range(1, side):
            leaf_sum_copy(k).wait()
            total = total + leaf_sum_in[k]
        value_own[...] = -total[:leaf_part] / (total[leaf_part:] + DAMPING)
        for k in range(1, side):
            value_copy(k).start()

    def leaf_third():
        for k in range(1, side):
            value_copy(k).wait()
        who = lax.broadcasted_iota(jnp.int32, (leaves, label_count), 0) // leaf_part
        found = jnp.zeros((leaves, label_count), jnp.float32)
        for k in range(side):
            owner = (me_y - k + side) % side
            row = value_own[...] if k == 0 else value_in[k]
            tiled = jnp.concatenate([row] * side, axis=0)
            found = jnp.where(who == owner, tiled, found)
        high = found.astype(jnp.bfloat16).astype(jnp.float32)
        rest = found - high
        middle = rest.astype(jnp.bfloat16).astype(jnp.float32)
        pad = jnp.zeros((128 - 3 * leaves, label_count), jnp.float32)
        values[...] = jnp.concatenate([high, middle, rest - middle, pad], 0).astype(jnp.bfloat16)

    def stored(c):
        rows = pl.ds(c * CHUNK, CHUNK)
        return pltpu.make_async_copy(newp.at[rows], newp_hbm.at[rows], store_sem.at[c])

    def update(c):
        rows = pl.ds(c * CHUNK, CHUNK)
        moved = jnp.dot(leaf_hot[rows, :], values[...], preferred_element_type=jnp.float32)
        newp[rows, :] = (pred[rows, :].astype(jnp.float32) + SHRINKAGE * moved).astype(
            jnp.bfloat16
        )
        stored(c).start()

    groups = len(GROUPS)
    for g in range(groups):
        compute(g)
        relay_start(g)
        if g == 2:
            leaf_first()
    for g in range(groups):
        relay_pass(g)
    leaf_second()
    for g in range(groups):
        finish(g)
        if g >= groups - 2:
            last_start(axis_of[g])
    leaf_third()
    for c in range(chunks):
        update(c)
    for g in range(groups - 2, groups):
        collect(axis_of[g])
    for c in range(chunks):
        stored(c).wait()


def copy_kernel(newp_in, hist_in, newp_out, hist_out, newp, hist, in_sem, out_sem):
    parts = in_sem.shape[0] - 1
    size = newp.shape[0] // parts
    moves = []
    for i in range(parts):
        rows = pl.ds(i * size, size)
        moves.append((newp_in.at[rows], newp.at[rows], newp_out.at[rows]))
    moves.append((hist_in, hist, hist_out))
    ins = [pltpu.make_async_copy(a, b, in_sem.at[i]) for i, (a, b, c) in enumerate(moves)]
    outs = [pltpu.make_async_copy(b, c, out_sem.at[i]) for i, (a, b, c) in enumerate(moves)]
    for copy in ins:
        copy.start()
    for come, go in zip(ins, outs):
        come.wait()
        go.start()
    for copy in outs:
        copy.wait()


def per_device(
    side,
    feat_total,
    predictions,
    targets,
    sketch_matrix,
    bin_codes,
    row_node,
    smaller,
    split_feature,
    split_bin,
):
    row_count, label_count = predictions.shape
    columns = sketch_matrix.shape[0]
    feats = bin_codes.shape[0]
    pairs = feats // 2
    groups = len(GROUPS)
    half = side // 2
    owned_bins = BINS // (side * side)
    leaves = 2 * smaller.shape[0]
    leaf_part = leaves // side
    chunks = row_count // CHUNK
    lane_parts = max(1, feat_total * 8 // columns)
    piece = (columns * lane_parts // feat_total, row_count // lane_parts)
    vmem = pltpu.VMEM
    bf16, f32, i32, f8 = jnp.bfloat16, jnp.float32, jnp.int32, jnp.float8_e4m3fn
    dma = pltpu.SemaphoreType.DMA
    whole = pl.BlockSpec(memory_space=pltpu.VMEM)
    scalar = pl.BlockSpec(memory_space=pltpu.SMEM)
    far = pl.BlockSpec(memory_space=pltpu.HBM)
    wide_shape = (row_count, label_count)
    newp, histograms = pl.pallas_call(
        functools.partial(kernel, side, feat_total),
        out_shape=(
            jax.ShapeDtypeStruct(wide_shape, bf16),
            jax.ShapeDtypeStruct((owned_bins, pairs * 128), f32),
        ),
        in_specs=[far] * 5 + [scalar] * 3,
        out_specs=(far, whole),
        scratch_shapes=[
            vmem(wide_shape, bf16),
            vmem(wide_shape, bf16),
            vmem((columns, label_count), bf16),
            vmem((feats, row_count), i32),
            vmem((row_count,), i32),
            vmem(wide_shape, bf16),
            vmem(wide_shape, bf16),
            vmem((columns, row_count), f32),
            vmem((feat_total,) + piece, f32),
            vmem((columns, row_count), f32),
            vmem((1, row_count), f32),
            vmem((feat_total, 1, row_count), f32),
            vmem((2, row_count, 256), f8),
            vmem((feats, row_count), f32),
            vmem((2, BINS, 128), bf16),
            vmem((2, pairs, BINS, row_count), f8),
            vmem((pairs, BINS, 128), f32),
            vmem((groups, 2, half, WIDEST, BINS // side, 128), f32),
            vmem((2, side, pairs // 2, owned_bins, 128), f32),
            vmem((2, side, pairs // 2, owned_bins, 128), f32),
            vmem((side, 2 * leaf_part, label_count), f32),
            vmem((side, 2 * leaf_part, label_count), f32),
            vmem((2 * leaf_part, label_count), f32),
            vmem((side, 2 * leaf_part, label_count), f32),
            vmem((leaf_part, label_count), f32),
            vmem((side, leaf_part, label_count), f32),
            vmem((128, label_count), bf16),
            vmem((row_count, 128), bf16),
            vmem(wide_shape, bf16),
            dma((2, chunks)),
            dma((3,)),
            dma((chunks,)),
            dma((feat_total,)),
            dma((feat_total,)),
            dma((feat_total,)),
            dma((feat_total,)),
            dma((feat_total,)),
            dma((feat_total,)),
            dma((groups, 2, half)),
            dma((groups, 2, half)),
            dma((2, side)),
            dma((2, side)),
            dma((3, side)),
            dma((3, side)),
        ],
        compiler_params=pltpu.CompilerParams(
            collective_id=0, has_side_effects=True, vmem_limit_bytes=62 << 20
        ),
        name="boost",
    )(
        predictions,
        targets,
        sketch_matrix,
        bin_codes,
        row_node,
        smaller,
        split_feature,
        split_bin,
    )
    return pl.pallas_call(
        copy_kernel,
        out_shape=(
            jax.ShapeDtypeStruct(newp.shape, newp.dtype),
            jax.ShapeDtypeStruct(histograms.shape, histograms.dtype),
        ),
        in_specs=[far, far],
        out_specs=(far, far),
        scratch_shapes=[
            vmem(newp.shape, newp.dtype),
            vmem(histograms.shape, histograms.dtype),
            dma((chunks + 1,)),
            dma((chunks + 1,)),
        ],
        compiler_params=pltpu.CompilerParams(vmem_limit_bytes=62 << 20),
        name="hand_on",
    )(newp, histograms)


def solution(mesh):
    placed = (
        P("rows", "feat"),
        P("rows", "feat"),
        P(None, "feat"),
        P("feat", "rows"),
        P("rows"),
        P(),
        P(),
        P(),
    )
    side = math.isqrt(mesh.shape["rows"])
    return jax.shard_map(
        functools.partial(per_device, side, mesh.shape["feat"]),
        mesh=mesh,
        in_specs=placed,
        out_specs=(P("rows", "feat"), P("rows", "feat")),
        check_vma=False,
    )
```

```python
import functools
import math

import jax
import jax.numpy as jnp
from jax import lax
from jax.experimental import pallas as pl
from jax.experimental.pallas import tpu as pltpu
from jax.sharding import PartitionSpec as P

BINS = 256
DAMPING = 1.0
SHRINKAGE = 0.5
UNIT = 2
GROUPS = ((0, 0, 2), (1, 0, 2), (0, 2, 4), (1, 2, 4), (0, 6, 2), (1, 6, 2))
CHAINED = (0, 1, 2, 3)
WIDEST = 4
ROUNDS = ((0, 6), (6, 2))
LOWER = 16.0
CHUNK = 256
BLOCK = 64
MESH = pl.DeviceIdType.MESH


def kernel(
    side,
    feat_total,
    pred_hbm,
    targ_hbm,
    matrix_hbm,
    codes_hbm,
    node_hbm,
    smaller_ref,
    feature_ref,
    bin_ref,
    newp_hbm,
    hist_ref,
    pred,
    targ,
    matrix,
    codes,
    node_line,
    grad,
    hess,
    part,
    part_in,
    sketch,
    right,
    right_in,
    weights,
    lines,
    bins,
    one_hots,
    hist,
    ring_in,
    last_out,
    last_in,
    leaf_out,
    leaf_in,
    leaf_sum,
    leaf_sum_in,
    value_own,
    value_in,
    values,
    leaf_hot,
    newp,
    load_sem,
    small_sem,
    store_sem,
    right_send,
    right_recv,
    part_send,
    part_recv,
    sketch_send,
    sketch_recv,
    ring_send,
    ring_recv,
    last_send,
    last_recv,
    leaf_send,
    leaf_recv,
):
    row_count, label_count = grad.shape
    chunks = row_count // CHUNK
    feats = codes.shape[0]
    nodes = smaller_ref.shape[0]
    leaves = 2 * nodes
    per_axis = hist.shape[0] // 2
    half = side // 2
    owned_bins = BINS // (side * side)
    ring_bins = BINS // side
    leaf_part = leaves // side

    here = lax.axis_index("rows")
    me_z = here // side
    me_y = here % side
    me_f = lax.axis_index("feat")
    me_of = (me_y, me_z)

    def at_y(k):
        return {"rows": me_z * side + (me_y + k + side) % side}

    def at_z(k):
        return {"rows": ((me_z + k + side) % side) * side + me_y}

    at_of = (at_y, at_z)

    def at_f(k):
        return {"feat": (me_f + k) % feat_total}

    def remote(src, dst, send, recv, where):
        return pltpu.make_async_remote_copy(
            src_ref=src,
            dst_ref=dst,
            send_sem=send,
            recv_sem=recv,
            device_id=where,
            device_id_type=MESH,
        )

    def loads(c):
        rows = pl.ds(c * CHUNK, CHUNK)
        return (
            pltpu.make_async_copy(pred_hbm.at[rows], pred.at[rows], load_sem.at[0, c]),
            pltpu.make_async_copy(targ_hbm.at[rows], targ.at[rows], load_sem.at[1, c]),
        )

    small_loads = (
        pltpu.make_async_copy(node_hbm, node_line, small_sem.at[0]),
        pltpu.make_async_copy(codes_hbm, codes, small_sem.at[1]),
        pltpu.make_async_copy(matrix_hbm, matrix, small_sem.at[2]),
    )
    barrier = pltpu.get_barrier_semaphore()
    for k in range(1, feat_total):
        pl.semaphore_signal(barrier, inc=1, device_id=at_f(k), device_id_type=MESH)
    for k in range(1, side):
        pl.semaphore_signal(barrier, inc=1, device_id=at_y(k), device_id_type=MESH)
        pl.semaphore_signal(barrier, inc=1, device_id=at_z(k), device_id_type=MESH)
    for copy in small_loads:
        copy.start()
    for c in range(chunks):
        for copy in loads(c):
            copy.start()

    place = lax.broadcasted_iota(jnp.int32, (BINS, 128), 0)
    major, rest = place // ring_bins, place % ring_bins
    minor, low = rest // owned_bins, rest % owned_bins
    bins[0] = ((minor * side + major) * owned_bins + low).astype(jnp.float32).astype(jnp.bfloat16)
    bins[1] = place.astype(jnp.float32).astype(jnp.bfloat16)
    for copy in small_loads:
        copy.wait()

    def elementwise(c):
        for copy in loads(c):
            copy.wait()

        def block(b, carry):
            rows = pl.ds(pl.multiple_of(c * CHUNK + b * BLOCK, BLOCK), BLOCK)
            logits = pred[rows, :].astype(jnp.float32)
            prob = 0.5 * jnp.tanh(0.5 * logits) + 0.5
            grad[rows, :] = (prob - targ[rows, :].astype(jnp.float32)).astype(jnp.bfloat16)
            hess[rows, :] = (prob * (1.0 - prob)).astype(jnp.bfloat16)
            return carry

        lax.fori_loop(0, CHUNK // BLOCK, block, 0)
        rows = pl.ds(c * CHUNK, CHUNK)
        part[:, rows] = lax.dot_general(
            matrix[...],
            grad[rows, :],
            (((1,), (1,)), ((), ())),
            preferred_element_type=jnp.float32,
        )

    for c in range(chunks):
        elementwise(c)

    node = jnp.concatenate(
        [node_line[pl.ds(i * 128, 128)].reshape(1, 128) for i in range(row_count // 128)], axis=1
    )
    right_part = jnp.zeros((1, row_count), jnp.float32)
    for n in range(nodes):
        local = feature_ref[n] - me_f * feats
        mine = (local >= 0) & (local < feats)
        row = codes[pl.ds(jnp.clip(local, 0, feats - 1), 1), :]
        limit = jnp.where(mine, bin_ref[n], BINS)
        right_part += jnp.where((node == n) & (row > limit), 1.0, 0.0)
    right[...] = right_part

    piece_rows, piece_lanes = part_in.shape[1:]
    lane_parts = row_count // piece_lanes

    def piece(f):
        return (
            pl.ds(pl.multiple_of((f // lane_parts) * piece_rows, piece_rows), piece_rows),
            pl.ds(pl.multiple_of((f % lane_parts) * piece_lanes, 128), piece_lanes),
        )

    def right_copy(k):
        return remote(right, right_in.at[k], right_send.at[k], right_recv.at[k], at_f(k))

    def part_copy(k):
        return remote(
            part.at[piece((me_f + k) % feat_total)],
            part_in.at[k],
            part_send.at[k],
            part_recv.at[k],
            at_f(k),
        )

    def sketch_copy(k, owner):
        return remote(
            sketch.at[piece(owner)],
            sketch.at[piece(owner)],
            sketch_send.at[k],
            sketch_recv.at[k],
            at_f(k),
        )

    lines[...] = codes[...].astype(jnp.float32)

    def build(first, last):
        def one(f, carry):
            unit = f // (2 * UNIT)
            turn = unit % 2
            slot = turn * per_axis + unit // 2 * UNIT + f // 2 % UNIT
            row = lines[pl.ds(f, 1), :]
            tile = jnp.broadcast_to(row, (16, row_count)).astype(jnp.bfloat16)
            wanted = jnp.concatenate([tile] * (BINS // 16), axis=0)
            ids = jnp.concatenate([bins[turn]] * (row_count // 128), axis=1)
            hot = jnp.where(ids == wanted, jnp.bfloat16(1), jnp.bfloat16(0))
            one_hots[f % 2, slot] = hot.astype(one_hots.dtype)
            return carry

        lax.fori_loop(first, last, one, 0)

    third = feats // 4
    build(0, third)
    pl.semaphore_wait(barrier, feat_total - 1 + 2 * (side - 1))
    for k in range(1, feat_total):
        part_copy(k).start()
    for k in range(1, feat_total):
        right_copy(k).start()
    build(third, 3 * third)

    mine = part[piece(me_f)]
    for k in range(1, feat_total):
        part_copy(k).wait()
        mine = mine + part_in[k]
    sketch[piece(me_f)] = mine
    for k in range(1, feat_total):
        sketch_copy(k, me_f).start()

    side_of = right_part
    for k in range(1, feat_total):
        right_copy(k).wait()
        side_of = side_of + right_in[k]
    leaf_id = 2 * node + (side_of > 0.5).astype(jnp.int32)
    tall = lax.broadcasted_iota(jnp.int32, (128, row_count), 0)
    hot = jnp.where((tall % leaves == leaf_id) & (tall < 3 * leaves), 1.0, 0.0)
    wide = hot[:leaves].astype(jnp.bfloat16)
    grad_sum = jnp.dot(wide, grad[...], preferred_element_type=jnp.float32)
    hess_sum = jnp.dot(wide, hess[...], preferred_element_type=jnp.float32)
    for i in range(side):
        leaf_out[i, :leaf_part, :] = grad_sum[i * leaf_part : (i + 1) * leaf_part]
        leaf_out[i, leaf_part:, :] = hess_sum[i * leaf_part : (i + 1) * leaf_part]

    def leaf_copy(k):
        return remote(
            leaf_out.at[(me_y + k) % side],
            leaf_in.at[k],
            leaf_send.at[0, k],
            leaf_recv.at[0, k],
            at_y(k),
        )

    def leaf_sum_copy(k):
        return remote(
            leaf_sum, leaf_sum_in.at[k], leaf_send.at[1, k], leaf_recv.at[1, k], at_z(k)
        )

    def value_copy(k):
        return remote(value_own, value_in.at[k], leaf_send.at[2, k], leaf_recv.at[2, k], at_y(k))

    for k in range(1, side):
        leaf_copy(k).start()
    leaf_hot[...] = hot.T.astype(jnp.bfloat16)
    build(3 * third, feats)

    for k in range(1, feat_total):
        sketch_copy(k, me_f).wait_send()
        sketch_copy(k, (me_f - k + feat_total) % feat_total).wait_recv()

    full = sketch[...]
    slots = []
    for s in range(nodes // 2):
        keep = jnp.zeros((1, row_count), jnp.float32)
        for n in (2 * s, 2 * s + 1):
            keep += jnp.where((node == n) & (smaller_ref[n] == 1), 1.0, 0.0)
        slots.append(full * keep)
    picked = jnp.concatenate(slots, axis=0).astype(jnp.bfloat16).astype(jnp.float32)
    most = jnp.max(jnp.abs(picked), axis=(0, 1), keepdims=True)
    power = jnp.floor(jnp.log2(jnp.maximum(most, 1e-30)))
    scaled = picked * jnp.exp2(7.0 - power)
    upper = scaled.astype(jnp.bfloat16).astype(weights.dtype).astype(jnp.float32)
    lower = (scaled - upper) * LOWER
    turned = jnp.concatenate([upper, lower], axis=0).T
    swapped = pltpu.roll(turned, 64, 1)
    left_half = lax.broadcasted_iota(jnp.int32, turned.shape, 1) < 64
    tables = (
        (jnp.where(left_half, turned, 0.0), jnp.where(left_half, swapped, 0.0)),
        (jnp.where(left_half, 0.0, swapped), jnp.where(left_half, 0.0, turned)),
    )
    for i in (0, 1):
        for j in (0, 1):
            table = tables[i][j].astype(jnp.bfloat16)
            weights[i, :, j * 128 : (j + 1) * 128] = table.astype(weights.dtype)
    unscale = jnp.exp2(power - 7.0)

    axis_of = [axis for axis, _, _ in GROUPS]
    size_of = [size for _, _, size in GROUPS]
    start_of = [axis * per_axis + first for axis, first, _ in GROUPS]

    def pairs_of(g):
        return pl.ds(start_of[g], size_of[g])

    def compute(g):
        total = None
        for i in (0, 1):
            left = one_hots[i, pairs_of(g)].reshape(size_of[g] * BINS, row_count)
            product = jnp.dot(left, weights[i], preferred_element_type=jnp.float32)
            total = product if total is None else total + product
        total = (total[:, :128] + total[:, 128:] * (1.0 / LOWER)) * unscale
        hist[pairs_of(g)] = total.reshape(size_of[g], BINS, 128)

    def rows_of(target):
        return pl.ds(pl.multiple_of((target + side) % side * ring_bins, ring_bins), ring_bins)

    def pair_range(g, way, d):
        size = size_of[g]
        return (way * (size // 2), size // 2) if d == half else (0, size)

    relay = max(1, half // 2)

    def chained(g):
        return g in CHAINED and 1 < relay < half

    def hops(g, d):
        if d > relay:
            return d - relay
        return d - 1 if chained(g) and d == relay and d > 1 else d

    def relay_copy(g, way, d):
        sign = 1 - 2 * way
        start, count = pair_range(g, way, d)
        return remote(
            hist.at[pl.ds(start_of[g] + start, count), rows_of(me_of[axis_of[g]] + sign * d)],
            ring_in.at[g, way, d - 1, pl.ds(start, count)],
            ring_send.at[g, way, d - 1],
            ring_recv.at[g, way, d - 1],
            at_of[axis_of[g]](sign * hops(g, d)),
        )

    def relay_take(g, way, d, target):
        relay_copy(g, way, d).wait()
        start, count = pair_range(g, way, d)
        spot = (pl.ds(start_of[g] + start, count), rows_of(target), slice(None))
        hist[spot] = hist[spot] + ring_in[g, way, d - 1, start : start + count]

    def relay_start(g):
        for d in range(half, 0, -1):
            if (d > relay if chained(g) else d != relay) or relay == half:
                for way in (0, 1):
                    relay_copy(g, way, d).start()

    def relay_pass(g):
        if relay < half:
            for way, sign in ((0, 1), (1, -1)):
                for d in range(half, relay, -1):
                    relay_take(g, way, d, me_of[axis_of[g]] + sign * relay)
                relay_copy(g, way, relay).start()

    def chain_pass(g):
        if chained(g):
            for way, sign in ((0, 1), (1, -1)):
                relay_take(g, way, relay, me_of[axis_of[g]] + sign * (relay - 1))
                relay_copy(g, way, relay - 1).start()

    def relay_end(g):
        for d in range(1, relay if chained(g) else relay + 1):
            for way in (0, 1):
                relay_take(g, way, d, me_of[axis_of[g]])

    by_distance = sorted(range(1, side), key=lambda k: -min(k, side - k))

    def last_copy(c, part, k):
        spot = pl.ds(*ROUNDS[part])
        return remote(
            last_out.at[c, (me_of[1 - c] + k) % side, spot],
            last_in.at[c, k, spot],
            last_send.at[c, part, k],
            last_recv.at[c, part, k],
            at_of[1 - c](k),
        )

    def finish(g):
        relay_end(g)
        total = hist[pairs_of(g), rows_of(me_of[axis_of[g]]), :]
        spot = pl.ds(GROUPS[g][1], size_of[g])
        for i in range(side):
            last_out[axis_of[g], i, spot] = total[:, i * owned_bins : (i + 1) * owned_bins]

    def last_start(c, part):
        for k in by_distance:
            last_copy(c, part, k).start()

    def collect(c, part):
        first, count = ROUNDS[part]
        total = last_out[c, me_of[1 - c], first : first + count]
        for k in range(1, side):
            last_copy(c, part, k).wait()
            total = total + last_in[c, k, first : first + count]
        for i in range(first, first + count):
            pair = (i // UNIT * 2 + c) * UNIT + i % UNIT
            hist_ref[:, pair * 128 : (pair + 1) * 128] = total[i - first]

    def leaf_first():
        total = leaf_out[me_y]
        for k in range(1, side):
            leaf_copy(k).wait()
            total = total + leaf_in[k]
        leaf_sum[...] = total
        for k in range(1, side):
            leaf_sum_copy(k).start()

    def leaf_second():
        total = leaf_sum[...]
        for k in range(1, side):
            leaf_sum_copy(k).wait()
            total = total + leaf_sum_in[k]
        value_own[...] = -total[:leaf_part] / (total[leaf_part:] + DAMPING)
        for k in range(1, side):
            value_copy(k).start()

    def leaf_third():
        for k in range(1, side):
            value_copy(k).wait()
        who = lax.broadcasted_iota(jnp.int32, (leaves, label_count), 0) // leaf_part
        found = jnp.zeros((leaves, label_count), jnp.float32)
        for k in range(side):
            owner = (me_y - k + side) % side
            row = value_own[...] if k == 0 else value_in[k]
            tiled = jnp.concatenate([row] * side, axis=0)
            found = jnp.where(who == owner, tiled, found)
        high = found.astype(jnp.bfloat16).astype(jnp.float32)
        rest = found - high
        middle = rest.astype(jnp.bfloat16).astype(jnp.float32)
        pad = jnp.zeros((128 - 3 * leaves, label_count), jnp.float32)
        values[...] = jnp.concatenate([high, middle, rest - middle, pad], 0).astype(jnp.bfloat16)

    def stored(c):
        rows = pl.ds(c * CHUNK, CHUNK)
        return pltpu.make_async_copy(newp.at[rows], newp_hbm.at[rows], store_sem.at[c])

    def update(c):
        rows = pl.ds(c * CHUNK, CHUNK)
        moved = jnp.dot(leaf_hot[rows, :], values[...], preferred_element_type=jnp.float32)
        newp[rows, :] = (pred[rows, :].astype(jnp.float32) + SHRINKAGE * moved).astype(
            jnp.bfloat16
        )
        stored(c).start()

    groups = len(GROUPS)
    for g in range(groups):
        compute(g)
        relay_start(g)
        if g == 2:
            leaf_first()
    relay_pass(0)
    relay_pass(1)
    relay_pass(2)
    relay_pass(3)
    chain_pass(0)
    chain_pass(1)
    relay_pass(4)
    relay_pass(5)
    leaf_second()
    chain_pass(2)
    chain_pass(3)
    for g in range(groups):
        finish(g)
        if g >= groups - 4:
            last_start(axis_of[g], (g - groups + 4) // 2)
    leaf_third()
    for c in range(chunks):
        update(c)
    for part in range(2):
        for c in (0, 1):
            collect(c, part)
    for c in range(chunks):
        stored(c).wait()


def copy_kernel(newp_in, hist_in, newp_out, hist_out, newp, hist, in_sem, out_sem):
    parts = in_sem.shape[0] - 1
    size = newp.shape[0] // parts
    moves = []
    for i in range(parts):
        rows = pl.ds(i * size, size)
        moves.append((newp_in.at[rows], newp.at[rows], newp_out.at[rows]))
    moves.append((hist_in, hist, hist_out))
    ins = [pltpu.make_async_copy(a, b, in_sem.at[i]) for i, (a, b, c) in enumerate(moves)]
    outs = [pltpu.make_async_copy(b, c, out_sem.at[i]) for i, (a, b, c) in enumerate(moves)]
    for copy in ins:
        copy.start()
    for come, go in zip(ins, outs):
        come.wait()
        go.start()
    for copy in outs:
        copy.wait()


def per_device(
    side,
    feat_total,
    predictions,
    targets,
    sketch_matrix,
    bin_codes,
    row_node,
    smaller,
    split_feature,
    split_bin,
):
    row_count, label_count = predictions.shape
    columns = sketch_matrix.shape[0]
    feats = bin_codes.shape[0]
    pairs = feats // 2
    groups = len(GROUPS)
    half = side // 2
    owned_bins = BINS // (side * side)
    leaves = 2 * smaller.shape[0]
    leaf_part = leaves // side
    chunks = row_count // CHUNK
    lane_parts = max(1, feat_total * 8 // columns)
    piece = (columns * lane_parts // feat_total, row_count // lane_parts)
    vmem = pltpu.VMEM
    bf16, f32, i32, f8 = jnp.bfloat16, jnp.float32, jnp.int32, jnp.float8_e4m3fn
    dma = pltpu.SemaphoreType.DMA
    whole = pl.BlockSpec(memory_space=pltpu.VMEM)
    scalar = pl.BlockSpec(memory_space=pltpu.SMEM)
    far = pl.BlockSpec(memory_space=pltpu.HBM)
    wide_shape = (row_count, label_count)
    newp, histograms = pl.pallas_call(
        functools.partial(kernel, side, feat_total),
        out_shape=(
            jax.ShapeDtypeStruct(wide_shape, bf16),
            jax.ShapeDtypeStruct((owned_bins, pairs * 128), f32),
        ),
        in_specs=[far] * 5 + [scalar] * 3,
        out_specs=(far, whole),
        scratch_shapes=[
            vmem(wide_shape, bf16),
            vmem(wide_shape, bf16),
            vmem((columns, label_count), bf16),
            vmem((feats, row_count), i32),
            vmem((row_count,), i32),
            vmem(wide_shape, bf16),
            vmem(wide_shape, bf16),
            vmem((columns, row_count), f32),
            vmem((feat_total,) + piece, f32),
            vmem((columns, row_count), f32),
            vmem((1, row_count), f32),
            vmem((feat_total, 1, row_count), f32),
            vmem((2, row_count, 256), f8),
            vmem((feats, row_count), f32),
            vmem((2, BINS, 128), bf16),
            vmem((2, pairs, BINS, row_count), f8),
            vmem((pairs, BINS, 128), f32),
            vmem((groups, 2, half, WIDEST, BINS // side, 128), f32),
            vmem((2, side, pairs // 2, owned_bins, 128), f32),
            vmem((2, side, pairs // 2, owned_bins, 128), f32),
            vmem((side, 2 * leaf_part, label_count), f32),
            vmem((side, 2 * leaf_part, label_count), f32),
            vmem((2 * leaf_part, label_count), f32),
            vmem((side, 2 * leaf_part, label_count), f32),
            vmem((leaf_part, label_count), f32),
            vmem((side, leaf_part, label_count), f32),
            vmem((128, label_count), bf16),
            vmem((row_count, 128), bf16),
            vmem(wide_shape, bf16),
            dma((2, chunks)),
            dma((3,)),
            dma((chunks,)),
            dma((feat_total,)),
            dma((feat_total,)),
            dma((feat_total,)),
            dma((feat_total,)),
            dma((feat_total,)),
            dma((feat_total,)),
            dma((groups, 2, half)),
            dma((groups, 2, half)),
            dma((2, len(ROUNDS), side)),
            dma((2, len(ROUNDS), side)),
            dma((3, side)),
            dma((3, side)),
        ],
        compiler_params=pltpu.CompilerParams(
            collective_id=0, has_side_effects=True, vmem_limit_bytes=62 << 20
        ),
        name="boost",
    )(
        predictions,
        targets,
        sketch_matrix,
        bin_codes,
        row_node,
        smaller,
        split_feature,
        split_bin,
    )
    return pl.pallas_call(
        copy_kernel,
        out_shape=(
            jax.ShapeDtypeStruct(newp.shape, newp.dtype),
            jax.ShapeDtypeStruct(histograms.shape, histograms.dtype),
        ),
        in_specs=[far, far],
        out_specs=(far, far),
        scratch_shapes=[
            vmem(newp.shape, newp.dtype),
            vmem(histograms.shape, histograms.dtype),
            dma((chunks + 1,)),
            dma((chunks + 1,)),
        ],
        compiler_params=pltpu.CompilerParams(vmem_limit_bytes=62 << 20),
        name="hand_on",
    )(newp, histograms)


def solution(mesh):
    placed = (
        P("rows", "feat"),
        P("rows", "feat"),
        P(None, "feat"),
        P("feat", "rows"),
        P("rows"),
        P(),
        P(),
        P(),
    )
    side = math.isqrt(mesh.shape["rows"])
    return jax.shard_map(
        functools.partial(per_device, side, mesh.shape["feat"]),
        mesh=mesh,
        in_specs=placed,
        out_specs=(P("rows", "feat"), P("rows", "feat")),
        check_vma=False,
    )
```

```python
import functools
import math

import jax
import jax.numpy as jnp
from jax import lax
from jax.experimental import pallas as pl
from jax.experimental.pallas import tpu as pltpu
from jax.sharding import PartitionSpec as P

BINS = 256
DAMPING = 1.0
SHRINKAGE = 0.5
UNIT = 2
GROUPS = ((0, 0, 2), (1, 0, 2), (0, 2, 4), (1, 2, 4), (0, 6, 2), (1, 6, 2))
CHAINED = (0, 1, 2, 3)
WIDEST = 4
ROUNDS = ((0, 6), (6, 2))
LOWER = 16.0
CHUNK = 256
BLOCK = 64
MESH = pl.DeviceIdType.MESH


def kernel(
    side,
    feat_total,
    pred_hbm,
    targ_hbm,
    matrix_hbm,
    codes_hbm,
    node_hbm,
    smaller_ref,
    feature_ref,
    bin_ref,
    newp_hbm,
    hist_ref,
    pred,
    targ,
    matrix,
    codes,
    node_line,
    grad,
    hess,
    part,
    part_in,
    sketch,
    right,
    right_in,
    weights,
    lines,
    bins,
    one_hots,
    hist,
    ring_in,
    last_out,
    last_in,
    leaf_out,
    leaf_in,
    leaf_sum,
    leaf_sum_in,
    value_own,
    value_in,
    values,
    leaf_hot,
    newp,
    load_sem,
    small_sem,
    store_sem,
    right_send,
    right_recv,
    part_send,
    part_recv,
    sketch_send,
    sketch_recv,
    ring_send,
    ring_recv,
    last_send,
    last_recv,
    leaf_send,
    leaf_recv,
):
    row_count, label_count = grad.shape
    chunks = row_count // CHUNK
    feats = codes.shape[0]
    nodes = smaller_ref.shape[0]
    leaves = 2 * nodes
    per_axis = hist.shape[0] // 2
    half = side // 2
    owned_bins = BINS // (side * side)
    ring_bins = BINS // side
    leaf_part = leaves // side

    here = lax.axis_index("rows")
    me_z = here // side
    me_y = here % side
    me_f = lax.axis_index("feat")
    me_of = (me_y, me_z)

    def at_y(k):
        return {"rows": me_z * side + (me_y + k + side) % side}

    def at_z(k):
        return {"rows": ((me_z + k + side) % side) * side + me_y}

    at_of = (at_y, at_z)

    def at_f(k):
        return {"feat": (me_f + k) % feat_total}

    def remote(src, dst, send, recv, where):
        return pltpu.make_async_remote_copy(
            src_ref=src,
            dst_ref=dst,
            send_sem=send,
            recv_sem=recv,
            device_id=where,
            device_id_type=MESH,
        )

    def loads(c):
        rows = pl.ds(c * CHUNK, CHUNK)
        return (
            pltpu.make_async_copy(pred_hbm.at[rows], pred.at[rows], load_sem.at[0, c]),
            pltpu.make_async_copy(targ_hbm.at[rows], targ.at[rows], load_sem.at[1, c]),
        )

    small_loads = (
        pltpu.make_async_copy(node_hbm, node_line, small_sem.at[0]),
        pltpu.make_async_copy(codes_hbm, codes, small_sem.at[1]),
        pltpu.make_async_copy(matrix_hbm, matrix, small_sem.at[2]),
    )
    barrier = pltpu.get_barrier_semaphore()
    by_distance = sorted(range(1, side), key=lambda k: -min(k, side - k))
    feat_order = sorted(range(1, feat_total), key=lambda k: -min(k, feat_total - k))
    for k in by_distance:
        pl.semaphore_signal(barrier, inc=1, device_id=at_y(k), device_id_type=MESH)
        pl.semaphore_signal(barrier, inc=1, device_id=at_z(k), device_id_type=MESH)
    for k in feat_order:
        pl.semaphore_signal(barrier, inc=1, device_id=at_f(k), device_id_type=MESH)
    for copy in small_loads:
        copy.start()
    for c in range(chunks):
        for copy in loads(c):
            copy.start()

    place = lax.broadcasted_iota(jnp.int32, (BINS, 128), 0)
    major, rest = place // ring_bins, place % ring_bins
    minor, low = rest // owned_bins, rest % owned_bins
    bins[0] = ((minor * side + major) * owned_bins + low).astype(jnp.float32).astype(jnp.bfloat16)
    bins[1] = place.astype(jnp.float32).astype(jnp.bfloat16)
    for copy in small_loads:
        copy.wait()

    def elementwise(c):
        for copy in loads(c):
            copy.wait()

        def block(b, carry):
            rows = pl.ds(pl.multiple_of(c * CHUNK + b * BLOCK, BLOCK), BLOCK)
            logits = pred[rows, :].astype(jnp.float32)
            prob = 0.5 * jnp.tanh(0.5 * logits) + 0.5
            grad[rows, :] = (prob - targ[rows, :].astype(jnp.float32)).astype(jnp.bfloat16)
            hess[rows, :] = (prob * (1.0 - prob)).astype(jnp.bfloat16)
            return carry

        lax.fori_loop(0, CHUNK // BLOCK, block, 0)
        rows = pl.ds(c * CHUNK, CHUNK)
        part[:, rows] = lax.dot_general(
            matrix[...],
            grad[rows, :],
            (((1,), (1,)), ((), ())),
            preferred_element_type=jnp.float32,
        )

    for c in range(chunks):
        elementwise(c)

    node = jnp.concatenate(
        [node_line[pl.ds(i * 128, 128)].reshape(1, 128) for i in range(row_count // 128)], axis=1
    )
    right_part = jnp.zeros((1, row_count), jnp.float32)
    for n in range(nodes):
        local = feature_ref[n] - me_f * feats
        mine = (local >= 0) & (local < feats)
        row = codes[pl.ds(jnp.clip(local, 0, feats - 1), 1), :]
        limit = jnp.where(mine, bin_ref[n], BINS)
        right_part += jnp.where((node == n) & (row > limit), 1.0, 0.0)
    right[...] = right_part

    piece_rows, piece_lanes = part_in.shape[1:]
    lane_parts = row_count // piece_lanes

    def piece(f):
        return (
            pl.ds(pl.multiple_of((f // lane_parts) * piece_rows, piece_rows), piece_rows),
            pl.ds(pl.multiple_of((f % lane_parts) * piece_lanes, 128), piece_lanes),
        )

    def right_copy(k):
        return remote(right, right_in.at[k], right_send.at[k], right_recv.at[k], at_f(k))

    def part_copy(k):
        return remote(
            part.at[piece((me_f + k) % feat_total)],
            part_in.at[k],
            part_send.at[k],
            part_recv.at[k],
            at_f(k),
        )

    def sketch_copy(k, owner):
        return remote(
            sketch.at[piece(owner)],
            sketch.at[piece(owner)],
            sketch_send.at[k],
            sketch_recv.at[k],
            at_f(k),
        )

    lines[...] = codes[...].astype(jnp.float32)

    def build(first, last):
        def one(f, carry):
            unit = f // (2 * UNIT)
            turn = unit % 2
            slot = turn * per_axis + unit // 2 * UNIT + f // 2 % UNIT
            row = lines[pl.ds(f, 1), :]
            tile = jnp.broadcast_to(row, (16, row_count)).astype(jnp.bfloat16)
            wanted = jnp.concatenate([tile] * (BINS // 16), axis=0)
            ids = jnp.concatenate([bins[turn]] * (row_count // 128), axis=1)
            hot = jnp.where(ids == wanted, jnp.bfloat16(1), jnp.bfloat16(0))
            one_hots[f % 2, slot] = hot.astype(one_hots.dtype)
            return carry

        lax.fori_loop(first, last, one, 0)

    third = feats // 4
    build(0, third)
    pl.semaphore_wait(barrier, feat_total - 1 + 2 * (side - 1))
    for k in feat_order:
        part_copy(k).start()
    for k in range(1, feat_total):
        right_copy(k).start()
    build(third, 3 * third)

    mine = part[piece(me_f)]
    for k in range(1, feat_total):
        part_copy(k).wait()
        mine = mine + part_in[k]
    sketch[piece(me_f)] = mine
    for k in feat_order:
        sketch_copy(k, me_f).start()

    side_of = right_part
    for k in range(1, feat_total):
        right_copy(k).wait()
        side_of = side_of + right_in[k]
    leaf_id = 2 * node + (side_of > 0.5).astype(jnp.int32)
    tall = lax.broadcasted_iota(jnp.int32, (128, row_count), 0)
    hot = jnp.where((tall % leaves == leaf_id) & (tall < 3 * leaves), 1.0, 0.0)
    wide = hot[:leaves].astype(jnp.bfloat16)
    grad_sum = jnp.dot(wide, grad[...], preferred_element_type=jnp.float32)
    hess_sum = jnp.dot(wide, hess[...], preferred_element_type=jnp.float32)
    for i in range(side):
        leaf_out[i, :leaf_part, :] = grad_sum[i * leaf_part : (i + 1) * leaf_part]
        leaf_out[i, leaf_part:, :] = hess_sum[i * leaf_part : (i + 1) * leaf_part]

    def leaf_copy(k):
        return remote(
            leaf_out.at[(me_y + k) % side],
            leaf_in.at[k],
            leaf_send.at[0, k],
            leaf_recv.at[0, k],
            at_y(k),
        )

    def leaf_sum_copy(k):
        return remote(
            leaf_sum, leaf_sum_in.at[k], leaf_send.at[1, k], leaf_recv.at[1, k], at_z(k)
        )

    def value_copy(k):
        return remote(value_own, value_in.at[k], leaf_send.at[2, k], leaf_recv.at[2, k], at_y(k))

    for k in by_distance:
        leaf_copy(k).start()
    leaf_hot[...] = hot.T.astype(jnp.bfloat16)
    build(3 * third, feats)

    for k in range(1, feat_total):
        sketch_copy(k, me_f).wait_send()
        sketch_copy(k, (me_f - k + feat_total) % feat_total).wait_recv()

    full = sketch[...]
    slots = []
    for s in range(nodes // 2):
        keep = jnp.zeros((1, row_count), jnp.float32)
        for n in (2 * s, 2 * s + 1):
            keep += jnp.where((node == n) & (smaller_ref[n] == 1), 1.0, 0.0)
        slots.append(full * keep)
    picked = jnp.concatenate(slots, axis=0).astype(jnp.bfloat16).astype(jnp.float32)
    most = jnp.max(jnp.abs(picked), axis=(0, 1), keepdims=True)
    power = jnp.floor(jnp.log2(jnp.maximum(most, 1e-30)))
    scaled = picked * jnp.exp2(7.0 - power)
    upper = scaled.astype(jnp.bfloat16).astype(weights.dtype).astype(jnp.float32)
    lower = (scaled - upper) * LOWER
    turned = jnp.concatenate([upper, lower], axis=0).T
    swapped = pltpu.roll(turned, 64, 1)
    left_half = lax.broadcasted_iota(jnp.int32, turned.shape, 1) < 64
    tables = (
        (jnp.where(left_half, turned, 0.0), jnp.where(left_half, swapped, 0.0)),
        (jnp.where(left_half, 0.0, swapped), jnp.where(left_half, 0.0, turned)),
    )
    for i in (0, 1):
        for j in (0, 1):
            table = tables[i][j].astype(jnp.bfloat16)
            weights[i, :, j * 128 : (j + 1) * 128] = table.astype(weights.dtype)
    unscale = jnp.exp2(power - 7.0)

    axis_of = [axis for axis, _, _ in GROUPS]
    size_of = [size for _, _, size in GROUPS]
    start_of = [axis * per_axis + first for axis, first, _ in GROUPS]

    def pairs_of(g):
        return pl.ds(start_of[g], size_of[g])

    def compute(g):
        total = None
        for i in (0, 1):
            left = one_hots[i, pairs_of(g)].reshape(size_of[g] * BINS, row_count)
            product = jnp.dot(left, weights[i], preferred_element_type=jnp.float32)
            total = product if total is None else total + product
        total = (total[:, :128] + total[:, 128:] * (1.0 / LOWER)) * unscale
        hist[pairs_of(g)] = total.reshape(size_of[g], BINS, 128)

    def rows_of(target):
        return pl.ds(pl.multiple_of((target + side) % side * ring_bins, ring_bins), ring_bins)

    def pair_range(g, way, d):
        size = size_of[g]
        return (way * (size // 2), size // 2) if d == half else (0, size)

    relay = max(1, half // 2)

    def chained(g):
        return g in CHAINED and 1 < relay < half

    def hops(g, d):
        if d > relay:
            return d - relay
        return d - 1 if chained(g) and d == relay and d > 1 else d

    def relay_copy(g, way, d):
        sign = 1 - 2 * way
        start, count = pair_range(g, way, d)
        return remote(
            hist.at[pl.ds(start_of[g] + start, count), rows_of(me_of[axis_of[g]] + sign * d)],
            ring_in.at[g, way, d - 1, pl.ds(start, count)],
            ring_send.at[g, way, d - 1],
            ring_recv.at[g, way, d - 1],
            at_of[axis_of[g]](sign * hops(g, d)),
        )

    def relay_take(g, way, d, target):
        relay_copy(g, way, d).wait()
        start, count = pair_range(g, way, d)
        spot = (pl.ds(start_of[g] + start, count), rows_of(target), slice(None))
        hist[spot] = hist[spot] + ring_in[g, way, d - 1, start : start + count]

    def relay_start(g):
        for d in range(half, 0, -1):
            if (d > relay if chained(g) else d != relay) or relay == half:
                for way in (0, 1):
                    relay_copy(g, way, d).start()

    def relay_pass(g):
        if relay < half:
            for way, sign in ((0, 1), (1, -1)):
                for d in range(half, relay, -1):
                    relay_take(g, way, d, me_of[axis_of[g]] + sign * relay)
                relay_copy(g, way, relay).start()

    def chain_pass(g):
        if chained(g):
            for way, sign in ((0, 1), (1, -1)):
                relay_take(g, way, relay, me_of[axis_of[g]] + sign * (relay - 1))
                relay_copy(g, way, relay - 1).start()

    def relay_end(g):
        for d in range(1, relay if chained(g) else relay + 1):
            for way in (0, 1):
                relay_take(g, way, d, me_of[axis_of[g]])

    def last_copy(c, part, k):
        spot = pl.ds(*ROUNDS[part])
        return remote(
            last_out.at[c, (me_of[1 - c] + k) % side, spot],
            last_in.at[c, k, spot],
            last_send.at[c, part, k],
            last_recv.at[c, part, k],
            at_of[1 - c](k),
        )

    def finish(g):
        relay_end(g)
        total = hist[pairs_of(g), rows_of(me_of[axis_of[g]]), :]
        spot = pl.ds(GROUPS[g][1], size_of[g])
        for i in range(side):
            last_out[axis_of[g], i, spot] = total[:, i * owned_bins : (i + 1) * owned_bins]

    def last_start(c, part):
        for k in by_distance:
            last_copy(c, part, k).start()

    def collect(c, part):
        first, count = ROUNDS[part]
        total = last_out[c, me_of[1 - c], first : first + count]
        for k in range(1, side):
            last_copy(c, part, k).wait()
            total = total + last_in[c, k, first : first + count]
        for i in range(first, first + count):
            pair = (i // UNIT * 2 + c) * UNIT + i % UNIT
            hist_ref[:, pair * 128 : (pair + 1) * 128] = total[i - first]

    def leaf_first():
        total = leaf_out[me_y]
        for k in range(1, side):
            leaf_copy(k).wait()
            total = total + leaf_in[k]
        leaf_sum[...] = total
        for k in by_distance:
            leaf_sum_copy(k).start()

    def leaf_second():
        total = leaf_sum[...]
        for k in range(1, side):
            leaf_sum_copy(k).wait()
            total = total + leaf_sum_in[k]
        value_own[...] = -total[:leaf_part] / (total[leaf_part:] + DAMPING)
        for k in by_distance:
            value_copy(k).start()

    def leaf_third():
        for k in range(1, side):
            value_copy(k).wait()
        who = lax.broadcasted_iota(jnp.int32, (leaves, label_count), 0) // leaf_part
        found = jnp.zeros((leaves, label_count), jnp.float32)
        for k in range(side):
            owner = (me_y - k + side) % side
            row = value_own[...] if k == 0 else value_in[k]
            tiled = jnp.concatenate([row] * side, axis=0)
            found = jnp.where(who == owner, tiled, found)
        high = found.astype(jnp.bfloat16).astype(jnp.float32)
        rest = found - high
        middle = rest.astype(jnp.bfloat16).astype(jnp.float32)
        pad = jnp.zeros((128 - 3 * leaves, label_count), jnp.float32)
        values[...] = jnp.concatenate([high, middle, rest - middle, pad], 0).astype(jnp.bfloat16)

    def stored(c):
        rows = pl.ds(c * CHUNK, CHUNK)
        return pltpu.make_async_copy(newp.at[rows], newp_hbm.at[rows], store_sem.at[c])

    def update(c):
        rows = pl.ds(c * CHUNK, CHUNK)
        moved = jnp.dot(leaf_hot[rows, :], values[...], preferred_element_type=jnp.float32)
        newp[rows, :] = (pred[rows, :].astype(jnp.float32) + SHRINKAGE * moved).astype(
            jnp.bfloat16
        )
        stored(c).start()

    groups = len(GROUPS)
    for g in range(groups):
        compute(g)
        relay_start(g)
        if g == 2:
            leaf_first()
    relay_pass(0)
    relay_pass(1)
    relay_pass(2)
    relay_pass(3)
    chain_pass(0)
    chain_pass(1)
    relay_pass(4)
    relay_pass(5)
    leaf_second()
    chain_pass(2)
    chain_pass(3)
    for g in range(groups):
        finish(g)
        if g >= groups - 4:
            last_start(axis_of[g], (g - groups + 4) // 2)
    leaf_third()
    for c in range(chunks):
        update(c)
    for part in range(2):
        for c in (0, 1):
            collect(c, part)
    for c in range(chunks):
        stored(c).wait()


def copy_kernel(newp_in, hist_in, newp_out, hist_out, newp, hist, in_sem, out_sem):
    parts = in_sem.shape[0] - 1
    size = newp.shape[0] // parts
    moves = []
    for i in range(parts):
        rows = pl.ds(i * size, size)
        moves.append((newp_in.at[rows], newp.at[rows], newp_out.at[rows]))
    moves.append((hist_in, hist, hist_out))
    ins = [pltpu.make_async_copy(a, b, in_sem.at[i]) for i, (a, b, c) in enumerate(moves)]
    outs = [pltpu.make_async_copy(b, c, out_sem.at[i]) for i, (a, b, c) in enumerate(moves)]
    for copy in ins:
        copy.start()
    for come, go in zip(ins, outs):
        come.wait()
        go.start()
    for copy in outs:
        copy.wait()


def per_device(
    side,
    feat_total,
    predictions,
    targets,
    sketch_matrix,
    bin_codes,
    row_node,
    smaller,
    split_feature,
    split_bin,
):
    row_count, label_count = predictions.shape
    columns = sketch_matrix.shape[0]
    feats = bin_codes.shape[0]
    pairs = feats // 2
    groups = len(GROUPS)
    half = side // 2
    owned_bins = BINS // (side * side)
    leaves = 2 * smaller.shape[0]
    leaf_part = leaves // side
    chunks = row_count // CHUNK
    lane_parts = max(1, feat_total * 8 // columns)
    piece = (columns * lane_parts // feat_total, row_count // lane_parts)
    vmem = pltpu.VMEM
    bf16, f32, i32, f8 = jnp.bfloat16, jnp.float32, jnp.int32, jnp.float8_e4m3fn
    dma = pltpu.SemaphoreType.DMA
    whole = pl.BlockSpec(memory_space=pltpu.VMEM)
    scalar = pl.BlockSpec(memory_space=pltpu.SMEM)
    far = pl.BlockSpec(memory_space=pltpu.HBM)
    wide_shape = (row_count, label_count)
    newp, histograms = pl.pallas_call(
        functools.partial(kernel, side, feat_total),
        out_shape=(
            jax.ShapeDtypeStruct(wide_shape, bf16),
            jax.ShapeDtypeStruct((owned_bins, pairs * 128), f32),
        ),
        in_specs=[far] * 5 + [scalar] * 3,
        out_specs=(far, whole),
        scratch_shapes=[
            vmem(wide_shape, bf16),
            vmem(wide_shape, bf16),
            vmem((columns, label_count), bf16),
            vmem((feats, row_count), i32),
            vmem((row_count,), i32),
            vmem(wide_shape, bf16),
            vmem(wide_shape, bf16),
            vmem((columns, row_count), f32),
            vmem((feat_total,) + piece, f32),
            vmem((columns, row_count), f32),
            vmem((1, row_count), f32),
            vmem((feat_total, 1, row_count), f32),
            vmem((2, row_count, 256), f8),
            vmem((feats, row_count), f32),
            vmem((2, BINS, 128), bf16),
            vmem((2, pairs, BINS, row_count), f8),
            vmem((pairs, BINS, 128), f32),
            vmem((groups, 2, half, WIDEST, BINS // side, 128), f32),
            vmem((2, side, pairs // 2, owned_bins, 128), f32),
            vmem((2, side, pairs // 2, owned_bins, 128), f32),
            vmem((side, 2 * leaf_part, label_count), f32),
            vmem((side, 2 * leaf_part, label_count), f32),
            vmem((2 * leaf_part, label_count), f32),
            vmem((side, 2 * leaf_part, label_count), f32),
            vmem((leaf_part, label_count), f32),
            vmem((side, leaf_part, label_count), f32),
            vmem((128, label_count), bf16),
            vmem((row_count, 128), bf16),
            vmem(wide_shape, bf16),
            dma((2, chunks)),
            dma((3,)),
            dma((chunks,)),
            dma((feat_total,)),
            dma((feat_total,)),
            dma((feat_total,)),
            dma((feat_total,)),
            dma((feat_total,)),
            dma((feat_total,)),
            dma((groups, 2, half)),
            dma((groups, 2, half)),
            dma((2, len(ROUNDS), side)),
            dma((2, len(ROUNDS), side)),
            dma((3, side)),
            dma((3, side)),
        ],
        compiler_params=pltpu.CompilerParams(
            collective_id=0, has_side_effects=True, vmem_limit_bytes=62 << 20
        ),
        name="boost",
    )(
        predictions,
        targets,
        sketch_matrix,
        bin_codes,
        row_node,
        smaller,
        split_feature,
        split_bin,
    )
    return pl.pallas_call(
        copy_kernel,
        out_shape=(
            jax.ShapeDtypeStruct(newp.shape, newp.dtype),
            jax.ShapeDtypeStruct(histograms.shape, histograms.dtype),
        ),
        in_specs=[far, far],
        out_specs=(far, far),
        scratch_shapes=[
            vmem(newp.shape, newp.dtype),
            vmem(histograms.shape, histograms.dtype),
            dma((chunks + 1,)),
            dma((chunks + 1,)),
        ],
        compiler_params=pltpu.CompilerParams(vmem_limit_bytes=62 << 20),
        name="hand_on",
    )(newp, histograms)


def solution(mesh):
    placed = (
        P("rows", "feat"),
        P("rows", "feat"),
        P(None, "feat"),
        P("feat", "rows"),
        P("rows"),
        P(),
        P(),
        P(),
    )
    side = math.isqrt(mesh.shape["rows"])
    return jax.shard_map(
        functools.partial(per_device, side, mesh.shape["feat"]),
        mesh=mesh,
        in_specs=placed,
        out_specs=(P("rows", "feat"), P("rows", "feat")),
        check_vma=False,
    )
```
